512 devices in a mesh: gx: 16 (over y, x_hi, core), gy: 32 (over z, x_lo).
Axes of the slice: x: 4 (x_hi: 2, x_lo: 2; x = x_hi * 2 + x_lo), y: 4, z: 16, core: 2. Of those that a mesh axis runs over, the one named last changes fastest.
Arguments:
- features: bfloat16 [65536, 128], P(('gx', 'gy'))
- positions: float32 [3, 65536], P(None, ('gx', 'gy')), as said below
- wave_vectors: int32 [3, 16384], replicated, may hold values from -24 to 24, as said below
- filter_width: float32 [16], replicated, may hold values from 0.002 to 0.02
- w_charge: bfloat16 [128, 16], replicated, may hold values from -0.5 to 0.5
- w_filter_in: bfloat16 [20, 128], replicated, may hold values from -1.25 to 1.25
- filter_output_weight: bfloat16 [128, 128], replicated, may hold values from -0.5 to 0.5
- update_weight: bfloat16 [128, 128], replicated, may hold values from -0.125 to 0.125
- w_long: float32 [16, 128], replicated, may hold values from -1.5 to 1.5
- send_along_x: int32 [2, 16384], P(None, ('gx', 'gy')), may hold values from 0 to 127, as said below
- send_along_y: int32 [2, 16384], P(None, ('gx', 'gy')), may hold values from 0 to 191, as said below
- neighbours: int32 [64, 65536], P(None, ('gx', 'gy')), may hold values from 0 to 255
- neighbour_count: int32 [65536], P(('gx', 'gy')), may hold values from 8 to 64, as said below
- distances: float32 [64, 65536], P(None, ('gx', 'gy')), may hold values from 0.8 to 4.8
Outputs:
- updated: bfloat16 [65536, 128], P(('gx', 'gy'))
- forces: float32 [3, 65536], P(None, ('gx', 'gy'))
The draws below stay inside these ranges and needn't reach their ends.
Inputs may be any that keep to these rules, and one draw needn't show every extreme that they name: `positions`: fractional coordinates; atom i lies inside the x-y cell of its domain, z below one half. `wave_vectors`: distinct integer triples with a first component of 1 to 24 and the others from -24 to 23. `send_along_x`: each list of a domain holds 32 distinct atoms of that domain. `send_along_y`: each list of a domain holds 32 distinct rows of that domain's first_table. `neighbours`: rows of the ghost table of the atom's domain; slots at or past neighbour_count are unused. `neighbour_count`: every domain has an atom with all 64 slots used.
All inputs are finite; a program needn't handle non-finite values.
Results may differ from the reference program's by a relative error of at most 0.0062.
Values may be sent and summed in bfloat16 or wider, within the bound.
A program may use at most 128 MiB of HBM per device.

```python
import math
import jax
import jax.numpy as jnp
from jax import lax

FEATURE_WIDTH = 128
C = 16
K = 16384
NRBF = 20
NEIGHBOUR_SLOTS = 64
DOMAIN_ATOMS = 128
GHOST_ROWS = 32
TOTAL_ATOMS = 65536
N_GX = 16
N_GY = 32


def draw_features(key, part):
    key = jax.random.fold_in(key, 1)
    key_spread, key_base, key_offset = jax.random.split(key, 3)
    ranking = jnp.arange(TOTAL_ATOMS, dtype=jnp.float32) / TOTAL_ATOMS
    spread = jax.random.uniform(key_spread, (TOTAL_ATOMS,), jnp.float32)
    scaling = 0.1 * jnp.exp(math.log(3.0) * ranking) * jnp.exp(math.log(10.0) * spread)
    base = jax.random.normal(key_base, (TOTAL_ATOMS, FEATURE_WIDTH), jnp.float32)
    offset = jax.random.uniform(key_offset, (FEATURE_WIDTH,), jnp.float32, -1.0, 1.0)
    return (scaling[:, None] * (base + offset[None, :])).astype(jnp.bfloat16)


def draw_positions(key, part):
    key = jax.random.fold_in(key, 2)
    key_x, key_y, key_z = jax.random.split(key, 3)
    domain = jnp.arange(TOTAL_ATOMS, dtype=jnp.int32) // DOMAIN_ATOMS
    cell_x = (domain // N_GY).astype(jnp.float32)
    cell_y = (domain % N_GY).astype(jnp.float32)
    along_x = (cell_x + jax.random.uniform(key_x, (TOTAL_ATOMS,), jnp.float32)) / N_GX
    along_y = (cell_y + jax.random.uniform(key_y, (TOTAL_ATOMS,), jnp.float32)) / N_GY
    height = jax.random.uniform(key_z, (TOTAL_ATOMS,), jnp.float32)
    along_z = 0.5 * height
    return jnp.stack([along_x, along_y, along_z]).astype(jnp.float32)


def draw_wave_vectors(key, part):
    key = jax.random.fold_in(key, 3)
    chosen = jax.random.permutation(key, 24 * 48 * 48)[:K].astype(jnp.int32)
    first = chosen // 2304 + 1
    rest = chosen % 2304
    second = rest // 48 - 24
    third = rest % 48 - 24
    return jnp.stack([first, second, third]).astype(jnp.int32)


def draw_lists(key, limit):
    block_list = TOTAL_ATOMS // DOMAIN_ATOMS
    keys = jax.random.split(key, 2 * block_list)
    chosen = jax.vmap(lambda single: jax.random.permutation(single, limit)[:GHOST_ROWS])(keys)
    return chosen.reshape(2, block_list * GHOST_ROWS).astype(jnp.int32)


def draw_send_along_x(key, part):
    key = jax.random.fold_in(key, 5)
    return draw_lists(key, DOMAIN_ATOMS)


def draw_send_along_y(key, part):
    key = jax.random.fold_in(key, 6)
    return draw_lists(key, DOMAIN_ATOMS + 2 * GHOST_ROWS)


def draw_neighbour_count(key, part):
    key = jax.random.fold_in(key, 4)
    key_total_count, key_pick = jax.random.split(key, 2)
    block_list = TOTAL_ATOMS // DOMAIN_ATOMS
    count_values = jax.random.randint(key_total_count, (block_list, DOMAIN_ATOMS), NEIGHBOUR_SLOTS // 8, NEIGHBOUR_SLOTS + 1)
    picked_rows = jax.random.randint(key_pick, (block_list, 1), 0, DOMAIN_ATOMS)
    count_values = jnp.where(jnp.arange(DOMAIN_ATOMS, dtype=jnp.int32)[None, :] == picked_rows, NEIGHBOUR_SLOTS, count_values)
    return count_values.reshape(TOTAL_ATOMS).astype(jnp.int32)


def with_ends(drawn, stream_key, low, top_value):
    longest = drawn.shape.index(max(drawn.shape))
    spots = []
    for shift in (0, 1):
        where = [jax.random.randint(jax.random.fold_in(stream_key, axis), (), 0, length) for axis, length in enumerate(drawn.shape)]
        where[longest] = (where[longest] + shift) % drawn.shape[longest]
        spots.append(tuple(where))
    return drawn.at[spots[0]].set(low).at[spots[1]].set(top_value)


def levels(key, extent, cuts, smallest, largest):
    gain, own = 1.0, jax.random.fold_in(key, 6)
    for position, blocks in cuts:
        draws = jnp.exp(jax.random.uniform(jax.random.fold_in(own, position), (blocks,), jnp.float32, smallest / len(cuts), largest / len(cuts)))
        gain = gain * jnp.repeat(draws, extent[position] // blocks).reshape([-1 if axis == position else 1 for axis in range(len(extent))])
    return gain


def scatter_about(stream_key, extent, scale, most, kind=jnp.bfloat16):
    result = scale * jax.random.normal(stream_key, extent, jnp.float32)
    return jnp.clip(result, min=-most, max=most).astype(kind)


def setup_inputs(seed: int = 0) -> dict:
    arg_keys = jax.random.split(jax.random.key(seed), 15)
    return {
        "features": draw_features(jax.random.fold_in(arg_keys[14], 71), 0),
        "positions": draw_positions(jax.random.fold_in(arg_keys[14], 71), 0),
        "wave_vectors": draw_wave_vectors(jax.random.fold_in(arg_keys[14], 71), 0),
        "filter_width": jnp.clip(jnp.exp(jax.random.uniform(arg_keys[3], (C,), jnp.float32, math.log(0.002), math.log(0.02))), 0.002, 0.02),
        "w_charge": scatter_about(arg_keys[4], (FEATURE_WIDTH, C), FEATURE_WIDTH ** -0.5, 0.5),
        "w_filter_in": scatter_about(arg_keys[5], (NRBF, FEATURE_WIDTH), NRBF ** -0.5, 1.25),
        "filter_output_weight": scatter_about(arg_keys[6], (FEATURE_WIDTH, FEATURE_WIDTH), FEATURE_WIDTH ** -0.5, 0.5),
        "update_weight": scatter_about(arg_keys[7], (FEATURE_WIDTH, FEATURE_WIDTH), (FEATURE_WIDTH * NEIGHBOUR_SLOTS // 4) ** -0.5, 0.125),
        "w_long": scatter_about(arg_keys[8], (C, FEATURE_WIDTH), C ** -0.5, 1.5, jnp.float32),
        "send_along_x": draw_send_along_x(jax.random.fold_in(arg_keys[14], 71), 0),
        "send_along_y": draw_send_along_y(jax.random.fold_in(arg_keys[14], 71), 0),
        "neighbours": with_ends(jax.random.randint(arg_keys[11], (NEIGHBOUR_SLOTS, TOTAL_ATOMS), 0, DOMAIN_ATOMS + 4 * GHOST_ROWS), jax.random.fold_in(arg_keys[11], 1), 0, (DOMAIN_ATOMS + 4 * GHOST_ROWS) - 1).astype(jnp.int32),
        "neighbour_count": draw_neighbour_count(jax.random.fold_in(arg_keys[14], 71), 0),
        "distances": jnp.clip(0.8 + 4 * jax.random.uniform(arg_keys[13], (NEIGHBOUR_SLOTS, TOTAL_ATOMS), jnp.float32) ** levels(arg_keys[13], (NEIGHBOUR_SLOTS, TOTAL_ATOMS), ((1, 512),), -0.2, 0.2), 0.8, 4.8),
    }


two_pi = 2.0 * math.pi
force_unit = 0.001

def shifted_softplus(value):
    return jax.nn.softplus(value) - math.log(2.0)

def phase_table(k_piece, coords):
    kf = k_piece.astype(jnp.float32)
    angle = two_pi * (kf[0][:, None] * coords[0][None, :] + kf[1][:, None] * coords[1][None, :] + kf[2][:, None] * coords[2][None, :])
    return jnp.stack([jnp.cos(angle), jnp.sin(angle)]).astype(jnp.bfloat16)

def build_coefficients(structure, k_piece, filter_width):
    kf = k_piece.astype(jnp.float32)
    squared = two_pi * two_pi * (kf[0] * kf[0] + kf[1] * kf[1] + 0.25 * kf[2] * kf[2])
    weight = jnp.exp(-0.5 * (filter_width * filter_width)[:, None] * squared[None, :]) * (two_pi * two_pi / squared)[None, :]
    filtered = structure * weight[:, None, :]
    pieces = [filtered]
    for axis_index in range(3):
        factor = two_pi * kf[axis_index]
        pieces.append(jnp.stack([factor * filtered[:, 1], -factor * filtered[:, 0]], axis=1))
    return jnp.concatenate(pieces, axis=0).astype(jnp.bfloat16)

def ghost_tables(features, send_along_x, send_along_y):
    grid = features.reshape(N_GX, N_GY, DOMAIN_ATOMS, FEATURE_WIDTH)
    pick = jax.vmap(jax.vmap(lambda rows, chosen: jnp.take(rows, chosen, axis=0)))
    lists_x = send_along_x.reshape(2, N_GX, N_GY, GHOST_ROWS)
    from_minus = jnp.roll(pick(grid, lists_x[0]), 1, axis=0)
    from_plus = jnp.roll(pick(grid, lists_x[1]), -1, axis=0)
    first_table = jnp.concatenate([grid, from_minus, from_plus], axis=2)
    lists_y = send_along_y.reshape(2, N_GX, N_GY, GHOST_ROWS)
    from_minus = jnp.roll(pick(first_table, lists_y[0]), 1, axis=1)
    from_plus = jnp.roll(pick(first_table, lists_y[1]), -1, axis=1)
    ghost_table = jnp.concatenate([first_table, from_minus, from_plus], axis=2)
    return ghost_table.reshape(N_GX * N_GY, DOMAIN_ATOMS + 4 * GHOST_ROWS, FEATURE_WIDTH)

def local_messages(ghost_table, neighbour_ids, live_count, distance, w_filter_in, filter_output_weight):
    centers = 5.0 * jnp.arange(NRBF, dtype=jnp.float32) / (NRBF - 1)
    sharpness = 0.02 * (NRBF - 1) * (NRBF - 1)
    offsets = distance[..., None] - centers
    radial_basis = jnp.exp(-sharpness * offsets * offsets).astype(jnp.bfloat16)
    hidden_features = shifted_softplus(jnp.dot(radial_basis.reshape(-1, NRBF), w_filter_in, preferred_element_type=jnp.float32)).astype(jnp.bfloat16)
    filter_values = jnp.dot(hidden_features, filter_output_weight, preferred_element_type=jnp.float32).reshape(NEIGHBOUR_SLOTS, DOMAIN_ATOMS, FEATURE_WIDTH)
    neighbour_rows = jnp.take(ghost_table, neighbour_ids, axis=0).astype(jnp.float32)
    slots = lax.broadcasted_iota(jnp.int32, neighbour_ids.shape, 0)
    envelope = jnp.where(slots < live_count[None, :], 0.5 * (jnp.cos(math.pi * distance / 5.0) + 1.0), 0.0)
    return lax.optimization_barrier(jnp.sum(envelope[..., None] * neighbour_rows * filter_values, axis=0))

def reference(features, positions, wave_vectors, filter_width, w_charge, w_filter_in, filter_output_weight, update_weight, w_long, send_along_x, send_along_y, neighbours, neighbour_count, distances):
    domain_list = N_GX * N_GY
    charges = jnp.dot(features, w_charge, preferred_element_type=jnp.float32).astype(jnp.bfloat16).T
    mean_charge = lax.optimization_barrier(jnp.sum(charges.astype(jnp.float32), axis=1)) / TOTAL_ATOMS
    charge_blocks = charges.reshape(C, domain_list, DOMAIN_ATOMS).transpose(1, 0, 2)
    coord_blocks = positions.reshape(3, domain_list, DOMAIN_ATOMS).transpose(1, 0, 2)
    unit_row = jnp.ones((1, DOMAIN_ATOMS), jnp.bfloat16)

    def add_block(running, pieces):
        block_charges, block_coords = pieces
        wave_table = phase_table(wave_vectors, block_coords).reshape(2 * K, DOMAIN_ATOMS)
        extended = jnp.concatenate([block_charges, unit_row], axis=0)
        return (running + jnp.dot(extended, wave_table.T, preferred_element_type=jnp.float32), None)
    raw, unused = lax.scan(add_block, jnp.zeros((C + 1, 2 * K), jnp.float32), (charge_blocks, coord_blocks))
    raw = raw.reshape(C + 1, 2, K)
    structure = raw[:C] - mean_charge[:, None, None] * raw[C][None]
    coefficients = build_coefficients(structure, wave_vectors, filter_width).reshape(4 * C, 2 * K)
    inv_root = 1.0 / math.sqrt(TOTAL_ATOMS)

    def project(block_coords):
        wave_table = phase_table(wave_vectors, block_coords).reshape(2 * K, DOMAIN_ATOMS)
        return jnp.dot(coefficients, wave_table, preferred_element_type=jnp.float32) * inv_root
    fields = lax.map(project, coord_blocks)
    tables = ghost_tables(features, send_along_x, send_along_y)
    identity_blocks = neighbours.reshape(NEIGHBOUR_SLOTS, domain_list, DOMAIN_ATOMS).transpose(1, 0, 2)
    distance_blocks = distances.reshape(NEIGHBOUR_SLOTS, domain_list, DOMAIN_ATOMS).transpose(1, 0, 2)
    count_blocks = neighbour_count.reshape(domain_list, DOMAIN_ATOMS)

    def domain_messages(pieces):
        table, ids, count_values, lengths = pieces
        return local_messages(table, ids, count_values, lengths, w_filter_in, filter_output_weight)
    messages = lax.map(domain_messages, (tables, identity_blocks, count_blocks, distance_blocks))
    messages = messages.reshape(TOTAL_ATOMS, FEATURE_WIDTH).astype(jnp.bfloat16)
    potentials = fields[:, :C].transpose(0, 2, 1).reshape(TOTAL_ATOMS, C)
    updated = features.astype(jnp.float32) + jnp.dot(messages, update_weight, preferred_element_type=jnp.float32)
    updated = updated + jnp.dot(potentials, w_long, precision=lax.Precision.HIGHEST)
    centred = charge_blocks.astype(jnp.float32) - mean_charge[None, :, None]
    field_parts = fields[:, C:].reshape(domain_list, 3, C, DOMAIN_ATOMS)
    forces = -force_unit * lax.optimization_barrier(jnp.sum(centred[:, None] * field_parts, axis=2))
    forces = forces.transpose(1, 0, 2).reshape(3, TOTAL_ATOMS)
    return (updated.astype(jnp.bfloat16), forces)
```

```python
import functools
import math

import jax
import jax.numpy as jnp
from jax import lax
from jax.experimental import pallas as pl
from jax.experimental.pallas import tpu as pltpu
from jax.sharding import PartitionSpec as P

f32 = jnp.float32
bf16 = jnp.bfloat16

GX = 16
GY = 32
XY = 16
NZ = 16
ATOMS = 128
C = 16
K = 16384
PIECE = 512
PIECES = K // PIECE
TILES = 8
SLOTS = 64
RAW = 24
GROUP = 4
LAG = 4

TWO_PI = 2.0 * math.pi
FORCE_UNIT = 0.001
MAGIC = 12582912.0

SIN_POLY = (-0.79116057, 3.59775961, -7.30781532, 4.44287955)
COS_POLY = (-1.72807912, 5.7151373, -6.97763258, 1.41420395)


def horner(u, poly):
    value = poly[0] * u + poly[1]
    for term in poly[2:]:
        value = value * u + term
    return value


def cos_sin_turns(turns):
    r = turns - ((turns + MAGIC) - MAGIC)
    u = r * r
    s = r * horner(u, SIN_POLY)
    c = horner(u, COS_POLY)
    return 1.0 - s * s, s * c


def dot(a, b, **kw):
    return jnp.dot(a, b, preferred_element_type=f32, **kw)


def dot_nt(a, b):
    return lax.dot_general(a, b, (((1,), (1,)), ((), ())), preferred_element_type=f32)


def kernel(
    feat, pos, wv, fw, wch, win, wout, wup, wlong, sx, sy, nbr, cnt, dist,
    upd_o, frc_o,
    W, CS, CR, XS, XR, ZS, ZR, FALL, QS, QA, QB, QC, TAB, GS,
    scr, scr2, xt_s, qe_s, qf_s, mean_s, env_s, own_s, wgt_s, gt_s, wint_s, woutt_s,
    qa_s, qa_r, qb_s, qb_r, qc_s, qc_r, g_s, g_r, c_s, c_r, x_s, x_r, z_s, z_r, f_s, f_r,
    a_s, a_r, b_s, b_r,
):
    gx = lax.axis_index("gx")
    gy = lax.axis_index("gy")
    h = lax.rem(gx, 2)
    z = gy // 2
    m = (gx // 4) * 4 + lax.rem(gx // 2, 2) * 2 + lax.rem(gy, 2)

    def xy_dev(i):
        return ((i // 4) * 4 + lax.rem(i // 2, 2) * 2 + h, z * 2 + lax.rem(i, 2))

    def z_dev(i):
        return (gx, i * 2 + lax.rem(gy, 2))

    sib = (gx + 1 - 2 * h, gy)

    def wrap(i):
        return lax.rem(i + 2 * XY, XY)

    x_up = (lax.rem(gx + 1, GX), gy)
    x_down = (lax.rem(gx + GX - 1, GX), gy)
    y_up = (gx, lax.rem(gy + 1, GY))
    y_down = (gx, lax.rem(gy + GY - 1, GY))

    def rcopy(src, dst, ssem, rsem, dev):
        return pltpu.make_async_remote_copy(
            src_ref=src, dst_ref=dst, send_sem=ssem, recv_sem=rsem,
            device_id=dev, device_id_type=pl.DeviceIdType.MESH,
        )

    barrier = pltpu.get_barrier_semaphore()

    def greet(dev):
        pl.semaphore_signal(barrier, inc=1, device_id=dev, device_id_type=pl.DeviceIdType.MESH)

    def greet_ring(i, carry):
        greet(xy_dev(wrap(m + i)))
        greet(z_dev(wrap(z + i)))
        return carry

    greet(sib)
    for dev in (x_up, x_down, y_up, y_down):
        greet(dev)
    lax.fori_loop(1, XY, greet_ring, 0)

    features = feat[...]
    scr[...] = jnp.zeros_like(scr)
    scr[:, 0:C] = wch[...].astype(f32)
    charges = dot(features, scr[...].astype(bf16)).astype(bf16).astype(f32)
    charges_t = charges.T
    row_id = lax.broadcasted_iota(jnp.int32, (32, ATOMS), 0)
    qf_s[...] = charges_t[0:C]
    qe_s[...] = jnp.where(row_id == C, 1.0, charges_t[0:32]).astype(bf16)
    QS[0] = jnp.broadcast_to(jnp.sum(charges_t[0:C], axis=1, keepdims=True), (C, 128))

    x3 = pos[...]
    xhi = x3.astype(bf16).astype(f32)
    xmid = (x3 - xhi).astype(bf16).astype(f32)
    xlo = (x3 - xhi) - xmid
    scr[...] = jnp.zeros_like(scr)
    scr[0:3, :] = xhi
    scr[8:11, :] = xmid
    scr[16:19, :] = xlo
    xt_s[...] = scr[...].T.astype(bf16)

    lane_iota = lax.broadcasted_iota(jnp.int32, (ATOMS, 32), 0)

    def pick(list_ref, d, base):
        scr[:, 0:32] = jnp.where(list_ref[d : d + 1, :] == lane_iota + base, 1.0, 0.0)
        return scr[...].T[0:32].astype(bf16)

    scr[...] = jnp.zeros_like(scr)
    TAB[0:ATOMS] = features
    for d in range(2):
        GS[d] = dot(pick(sx, d, 0), features).astype(bf16)

    pl.semaphore_wait(barrier, 5 + 2 * (XY - 1))

    ghost = [
        rcopy(GS.at[0], TAB.at[pl.ds(128, 32)], g_s.at[0], g_r.at[0], x_up),
        rcopy(GS.at[1], TAB.at[pl.ds(160, 32)], g_s.at[1], g_r.at[1], x_down),
        rcopy(GS.at[2], TAB.at[pl.ds(192, 32)], g_s.at[2], g_r.at[2], y_up),
        rcopy(GS.at[3], TAB.at[pl.ds(224, 32)], g_s.at[3], g_r.at[3], y_down),
    ]

    def qa_copy(i, slot):
        return rcopy(QS.at[0], QA.at[slot], qa_s.at[i], qa_r.at[slot], xy_dev(i))

    def qb_copy(i, slot):
        return rcopy(QS.at[1], QB.at[slot], qb_s.at[i], qb_r.at[slot], z_dev(i))

    qc_copy = rcopy(QS.at[2], QC, qc_s, qc_r, sib)

    def start_qa(i, carry):
        qa_copy(wrap(m + i), m).start()
        return carry

    lax.fori_loop(1, XY, start_qa, 0)
    ghost[0].start()
    ghost[1].start()

    def reduce_qa():
        def wait(i, carry):
            j = wrap(m - i)
            qa_copy(j, j).wait_recv()
            return carry

        lax.fori_loop(1, XY, wait, 0)
        QA[m] = QS[0]
        total = QA[0]
        for j in range(1, XY):
            total = total + QA[j]
        QS[1] = total

        def start(i, carry):
            qb_copy(wrap(z + i), z).start()
            return carry

        lax.fori_loop(1, NZ, start, 0)

    def reduce_qb():
        def wait(i, carry):
            j = wrap(z - i)
            qb_copy(j, j).wait_recv()
            return carry

        lax.fori_loop(1, NZ, wait, 0)
        QB[z] = QS[1]
        total = QB[0]
        for j in range(1, NZ):
            total = total + QB[j]
        QS[2] = total
        qc_copy.start()

    def reduce_qc():
        qc_copy.wait_recv()
        mean = (QS[2] + QC[...]) * (1.0 / (GX * GY * ATOMS))
        mean_s[...] = jnp.concatenate([mean] * (PIECE // 128), axis=1)

    def wave_piece(g):
        k3 = wv[:, pl.ds(pl.multiple_of(g * PIECE, PIECE), PIECE)].astype(f32)
        k8 = jnp.concatenate([k3, jnp.zeros((5, PIECE), f32)], axis=0)
        kb = jnp.concatenate([k8, k8, k8, jnp.zeros((8, PIECE), f32)], axis=0).astype(bf16)
        xt = xt_s[:, 0:32]
        qe = qe_s[...]
        raws = ([], [])
        for j in range(PIECE // 128):
            lanes = slice(j * 128, (j + 1) * 128)
            cos, sin = cos_sin_turns(dot(xt, kb[:, lanes]))
            for p, wave in enumerate((cos.astype(bf16), sin.astype(bf16))):
                W[g, p, :, lanes] = wave
                raws[p].append(dot(qe, wave))
        return [jnp.concatenate(raw, axis=1)[0:RAW] for raw in raws]

    def core_copy(i):
        return rcopy(CS.at[i], CR.at[i], c_s.at[i], c_r.at[i], sib)

    def other_half(s, carry):
        i = wrap(m + s)
        raw = wave_piece((1 - h) * XY + i)
        CS[i, 0] = raw[0]
        CS[i, 1] = raw[1]
        core_copy(i).start()
        return carry

    def xy_copy(i, slot):
        return rcopy(XS.at[i], XR.at[slot], x_s.at[i], x_r.at[slot], xy_dev(i))

    def own_terms(s):
        i = wrap(m + s)
        raw = wave_piece(h * XY + i)
        core_copy(i).wait_recv()
        mean = mean_s[...]
        terms = []
        for p in range(2):
            total = raw[p] + CR[i, p]
            terms.append(total[0:C] - mean * total[C : C + 1])
        return i, terms

    def own_half(s, carry):
        i, terms = own_terms(s)
        XS[i, 0:C] = terms[0].astype(bf16)
        XS[i, C : 2 * C] = terms[1].astype(bf16)
        xy_copy(i, m).start()
        return carry

    lax.fori_loop(1, 6, other_half, 0)
    reduce_qa()
    ghost[0].wait_recv()
    ghost[1].wait_recv()
    scr[...] = jnp.zeros_like(scr)
    for d in range(2):
        rows = dot(pick(sy, d, 0), TAB[0:128]) + dot(pick(sy, d, 128)[:, 0:64], TAB[128:192])
        GS[2 + d] = rows.astype(bf16)
    ghost[2].start()
    ghost[3].start()
    lax.fori_loop(6, 12, other_half, 0)
    reduce_qb()
    lax.fori_loop(12, 17, other_half, 0)
    reduce_qc()
    lax.fori_loop(1, XY, own_half, 0)
    i_own, terms = own_terms(0)
    XR[m, 0:C] = terms[0].astype(bf16)
    XR[m, C : 2 * C] = terms[1].astype(bf16)

    scr[...] = jnp.zeros_like(scr)
    scr[0:20, :] = win[...].astype(f32)
    wint_s[...] = scr[...].T.astype(bf16)
    woutt_s[...] = wout[...].astype(f32).T.astype(bf16)
    ghost[2].wait_recv()
    ghost[3].wait_recv()
    gt_s[:, 0:128] = TAB[0:128].astype(f32).T.astype(bf16)
    gt_s[:, 128:256] = TAB[128:256].astype(f32).T.astype(bf16)
    slot_id = lax.broadcasted_iota(jnp.int32, (SLOTS, ATOMS), 0)
    swing, _ = cos_sin_turns(dist[...] * 0.1)
    env_s[...] = jnp.where(slot_id < cnt[...], 0.5 * (swing + 1.0), 0.0)

    centre = lax.broadcasted_iota(jnp.int32, (32, ATOMS), 0).astype(f32) * (5.0 / 19.0)
    table_row = lax.broadcasted_iota(jnp.int32, (2 * ATOMS, ATOMS), 0)
    sharpness = 0.02 * 19.0 * 19.0

    def message_step(i, running):
        base = i * GROUP
        basis, hot = [], []
        for u in range(GROUP):
            offset = dist[pl.ds(base + u, 1), :] - centre
            basis.append(jnp.exp(-sharpness * offset * offset).astype(bf16))
            hot.append(jnp.where(nbr[pl.ds(base + u, 1), :] == table_row, 1.0, 0.0).astype(bf16))
        for u in range(0, GROUP, 2):
            pre = dot(wint_s[:, 0:32], jnp.concatenate(basis[u : u + 2], axis=1))
            hidden = jnp.log(0.5 * jnp.exp(pre) + 0.5).astype(bf16)
            filters = dot(woutt_s[...], hidden)
            rows = dot(gt_s[...], jnp.concatenate(hot[u : u + 2], axis=1))
            both = filters * rows
            running = (
                running
                + env_s[pl.ds(base + u, 1), :] * both[:, 0:128]
                + env_s[pl.ds(base + u + 1, 1), :] * both[:, 128:256]
            )
        return running

    steps = SLOTS // GROUP
    messages = lax.fori_loop(0, steps // 2, message_step, jnp.zeros((128, ATOMS), f32))

    def wait_xy(i, carry):
        j = wrap(m - i)
        xy_copy(j, j).wait_recv()
        return carry

    lax.fori_loop(1, XY, wait_xy, 0)
    for kb in range(4):
        lanes = slice(kb * 128, (kb + 1) * 128)
        for p in range(2):
            rows = slice(p * C, (p + 1) * C)
            total = XR[0, rows, lanes].astype(f32)
            for j in range(1, XY):
                total = total + XR[j, rows, lanes].astype(f32)
            ZS[2 * kb + p] = total.astype(bf16)

    def z_copy(i, slot):
        return rcopy(ZS.at[lax.rem(i, TILES)], ZR.at[slot], z_s.at[i], z_r.at[slot], z_dev(i))

    def start_z(i, carry):
        z_copy(wrap(z + i), z).start()
        return carry

    lax.fori_loop(1, NZ, start_z, 0)
    tile = lax.rem(z, TILES)
    ZR[z] = ZS[tile]

    g_own = h * XY + m
    k_tile = pl.multiple_of(g_own * PIECE + (tile // 2) * 128, 128)
    kt = wv[:, pl.ds(k_tile, 128)].astype(f32)
    q2 = (TWO_PI * TWO_PI) * (
        kt[0:1] * kt[0:1] + kt[1:2] * kt[1:2] + 0.25 * (kt[2:3] * kt[2:3])
    )
    eye = lax.broadcasted_iota(jnp.int32, (C, C), 0) == lax.broadcasted_iota(jnp.int32, (C, C), 1)
    width = jnp.sum(jnp.where(eye, jnp.broadcast_to(fw[...], (C, C)), 0.0), axis=1, keepdims=True)
    weight = jnp.exp(-0.5 * (width * width) * q2) * ((TWO_PI * TWO_PI) / q2)
    wgt_s[...] = weight

    messages = lax.fori_loop(steps // 2, (3 * steps) // 4, message_step, messages)

    def wait_z(i, carry):
        j = wrap(z - i)
        z_copy(j, j).wait_recv()
        return carry

    lax.fori_loop(1, NZ, wait_z, 0)
    total = ZR[0].astype(f32)
    for j in range(1, NZ):
        total = total + ZR[j].astype(f32)
    FALL[g_own, tile] = (total * wgt_s[...]).astype(bf16)

    def f_copy(delta, slot_tile, slot):
        return rcopy(
            FALL.at[g_own, slot_tile], FALL.at[g_own, slot_tile], f_s.at[slot], f_r.at[slot_tile],
            z_dev(wrap(z + delta)),
        )

    for n, delta in enumerate((1, -1, 2, -2, 3, -3, 4)):
        f_copy(delta, tile, n).start()
    messages = lax.fori_loop((3 * steps) // 4, steps, message_step, messages)

    def wait_f(i, carry):
        f_copy(1, lax.rem(tile + i, TILES), 0).wait_recv()
        return carry

    lax.fori_loop(1, TILES, wait_f, 0)

    def a_copy(i, slot):
        return rcopy(
            FALL.at[h * XY + slot], FALL.at[h * XY + slot], a_s.at[i], a_r.at[slot], xy_dev(i)
        )

    def b_copy(half, i):
        return rcopy(FALL.at[half * XY + i], FALL.at[half * XY + i], b_s.at[i], b_r.at[i], sib)

    b_copy(h, m).start()

    def start_a(i, carry):
        a_copy(wrap(m + i), m).start()
        return carry

    lax.fori_loop(1, XY, start_a, 0)

    def project(g, running):
        kf = wv[:, pl.ds(pl.multiple_of(g * PIECE, PIECE), PIECE)].astype(f32) * TWO_PI
        f0 = jnp.concatenate([FALL[g, 2 * kb] for kb in range(4)], axis=1)
        f1 = jnp.concatenate([FALL[g, 2 * kb + 1] for kb in range(4)], axis=1)
        f0w, f1w = f0.astype(f32), f1.astype(f32)
        first, second = [f0], [f1]
        for d in range(3):
            first.append((kf[d : d + 1] * f1w).astype(bf16))
            second.append((-kf[d : d + 1] * f0w).astype(bf16))
        running = running + dot_nt(jnp.concatenate(first, axis=0), W[g, 0])
        return running + dot_nt(jnp.concatenate(second, axis=0), W[g, 1])

    def near(i, running):
        j = wrap(m - i)
        a_copy(j, j).wait_recv()
        b_copy(h, j).start()
        return project(h * XY + j, running)

    def far(i, running):
        j = wrap(m - i)
        b_copy(1 - h, j).wait_recv()
        return project((1 - h) * XY + j, running)

    fields = project(g_own, jnp.zeros((4 * C, ATOMS), f32))
    fields = lax.fori_loop(1, LAG, near, fields)
    fields = lax.fori_loop(LAG, XY, lambda i, v: far(i - LAG, near(i, v)), fields)
    fields = lax.fori_loop(XY - LAG, XY, far, fields)
    fields = fields * (1.0 / math.sqrt(GX * GY * ATOMS))

    centred = qf_s[...] - mean_s[:, 0:128]
    for d in range(3):
        part = fields[(d + 1) * C : (d + 2) * C]
        frc_o[d : d + 1, :] = -FORCE_UNIT * jnp.sum(centred * part, axis=0, keepdims=True)
    scr[...] = jnp.zeros_like(scr)
    scr[0:C, :] = fields[0:C]
    scr2[...] = jnp.zeros_like(scr2)
    scr2[0:C, :] = wlong[...]
    long_part = dot(scr[...].T, scr2[...], precision=lax.Precision.HIGHEST)
    message_rows = messages.astype(bf16).astype(f32).T.astype(bf16)
    updated = features.astype(f32) + dot(message_rows, wup[...])
    upd_o[...] = (updated + long_part).astype(bf16)

    qc_copy.wait_send()
    for copy in ghost:
        copy.wait_send()

    def drain(i, carry):
        jm = wrap(m + i)
        jz = wrap(z + i)
        qa_copy(jm, m).wait_send()
        qb_copy(jz, z).wait_send()
        xy_copy(jm, m).wait_send()
        z_copy(jz, z).wait_send()
        a_copy(jm, m).wait_send()
        return carry

    lax.fori_loop(1, XY, drain, 0)

    def drain_core(i, carry):
        core_copy(i).wait_send()
        b_copy(h, i).wait_send()
        return carry

    lax.fori_loop(0, XY, drain_core, 0)
    for n in range(TILES - 1):
        f_copy(1, tile, n).wait_send()


def per_device(*args):
    feat, pos, wv, fw, wch, win, wout, wup, wlong, sx, sy, nbr, cnt, dist = args
    dma = pltpu.SemaphoreType.DMA
    scratch = [
        pltpu.VMEM((PIECES, 2, ATOMS, PIECE), bf16),
        pltpu.VMEM((XY, 2, RAW, PIECE), f32),
        pltpu.VMEM((XY, 2, RAW, PIECE), f32),
        pltpu.VMEM((XY, 2 * C, PIECE), bf16),
        pltpu.VMEM((XY, 2 * C, PIECE), bf16),
        pltpu.VMEM((TILES, C, 128), bf16),
        pltpu.VMEM((NZ, C, 128), bf16),
        pltpu.VMEM((PIECES, TILES, C, 128), bf16),
        pltpu.VMEM((3, C, 128), f32),
        pltpu.VMEM((XY, C, 128), f32),
        pltpu.VMEM((NZ, C, 128), f32),
        pltpu.VMEM((C, 128), f32),
        pltpu.VMEM((2 * ATOMS, 128), bf16),
        pltpu.VMEM((4, 32, 128), bf16),
        pltpu.VMEM((128, 128), f32),
        pltpu.VMEM((128, 128), f32),
        pltpu.VMEM((128, 128), bf16),
        pltpu.VMEM((32, ATOMS), bf16),
        pltpu.VMEM((C, ATOMS), f32),
        pltpu.VMEM((C, PIECE), f32),
        pltpu.VMEM((SLOTS, ATOMS), f32),
        pltpu.VMEM((8, 128), f32),
        pltpu.VMEM((C, 128), f32),
        pltpu.VMEM((128, 256), bf16),
        pltpu.VMEM((128, 128), bf16),
        pltpu.VMEM((128, 128), bf16),
        dma((XY,)), dma((XY,)), dma((NZ,)), dma((NZ,)), dma, dma,
        dma((4,)), dma((4,)),
        dma((XY,)), dma((XY,)),
        dma((XY,)), dma((XY,)),
        dma((NZ,)), dma((NZ,)),
        dma((TILES,)), dma((TILES,)),
        dma((XY,)), dma((XY,)),
        dma((XY,)), dma((XY,)),
    ]
    vmem = pl.BlockSpec(memory_space=pltpu.VMEM)
    return pl.pallas_call(
        kernel,
        out_shape=(
            jax.ShapeDtypeStruct((ATOMS, 128), bf16),
            jax.ShapeDtypeStruct((3, ATOMS), f32),
        ),
        in_specs=[vmem] * 14,
        out_specs=(vmem, vmem),
        scratch_shapes=scratch,
        compiler_params=pltpu.CompilerParams(
            collective_id=0, has_side_effects=True, vmem_limit_bytes=48 * 1024 * 1024
        ),
    )(
        feat, pos, wv, fw.reshape(1, C), wch, win, wout, wup, wlong, sx, sy, nbr,
        cnt.reshape(1, ATOMS), dist,
    )


def solution(mesh):
    atoms_first = P(("gx", "gy"), None)
    atoms_last = P(None, ("gx", "gy"))
    placed = (
        atoms_first, atoms_last, P(), P(), P(), P(), P(), P(), P(),
        atoms_last, atoms_last, atoms_last, P(("gx", "gy")), atoms_last,
    )
    return jax.shard_map(
        per_device,
        mesh=mesh,
        in_specs=placed,
        out_specs=(atoms_first, atoms_last),
        check_vma=False,
    )
```

```python
import functools
import math

import jax
import jax.numpy as jnp
from jax import lax
from jax.experimental import pallas as pl
from jax.experimental.pallas import tpu as pltpu
from jax.sharding import PartitionSpec as P

f32 = jnp.float32
bf16 = jnp.bfloat16

GX = 16
GY = 32
XY = 16
NZ = 16
ATOMS = 128
C = 16
K = 16384
PIECE = 512
PIECES = K // PIECE
TILES = 8
KBS = 4
SLOTS = 64
RAW = 24
GROUP = 8
LAG = 3

TWO_PI = 2.0 * math.pi
FORCE_UNIT = 0.001
MAGIC = 12582912.0

SIN_POLY = (-0.79116057, 3.59775961, -7.30781532, 4.44287955)
COS_POLY = (-1.72807912, 5.7151373, -6.97763258, 1.41420395)


def horner(u, poly):
    value = poly[0] * u + poly[1]
    for term in poly[2:]:
        value = value * u + term
    return value


def cos_sin_turns(turns):
    r = turns - ((turns + MAGIC) - MAGIC)
    u = r * r
    s = r * horner(u, SIN_POLY)
    c = horner(u, COS_POLY)
    return 1.0 - s * s, s * c


def dot(a, b, **kw):
    return jnp.dot(a, b, preferred_element_type=f32, **kw)


def dot_nt(a, b):
    return lax.dot_general(a, b, (((1,), (1,)), ((), ())), preferred_element_type=f32)


def kernel(*refs):
    sources, (upd_o, frc_o), held, rest = refs[:14], refs[14:16], refs[16:30], refs[30:]
    feat, pos, wv, fw, wch, win, wout, wup, wlong, sx, sy, nbr, cnt, dist = held
    (W, WA, WB, TA, TB, CS, CR, XS, XR, ZS, ZR, FALL, QS, QA, QB, QC, TAB, GS,
    scr, scr2, base_s, xt_s, qe_s, qf_s, mean_s, env_s, wgt_s, gt_s, wint_s, woutt_s,
    qa_s, qa_r, qb_s, qb_r, qc_s, qc_r, g_s, g_r, c_s, c_r, x_s, x_r, z_s, z_r, f_s, f_r,
    a_s, a_r, b_s, b_r, in_sem) = rest
    loads = [
        pltpu.make_async_copy(sources[n], held[n], in_sem.at[n]) for n in range(14)
    ]
    first_loads = (1, 2, 0, 4)
    later_loads = [n for n in range(14) if n not in first_loads]
    for n in first_loads:
        loads[n].start()
    gx = lax.axis_index("gx")
    gy = lax.axis_index("gy")
    h = lax.rem(gx, 2)
    z = gy // 2
    m = (gx // 4) * 4 + lax.rem(gx // 2, 2) * 2 + lax.rem(gy, 2)

    def xy_dev(i):
        return ((i // 4) * 4 + lax.rem(i // 2, 2) * 2 + h, z * 2 + lax.rem(i, 2))

    def z_dev(i):
        return (gx, i * 2 + lax.rem(gy, 2))

    sib = (gx + 1 - 2 * h, gy)

    def wrap(i):
        return lax.rem(i + 2 * XY, XY)

    def bend(a):
        return lax.rem(2 + a + a // 2 + 2 * (a // 3), 4)

    def xy_to(n):
        dy, dx = bend(n // 4), bend(lax.rem(n, 4))
        return lax.rem(m // 4 + dy, 4) * 4 + lax.rem(lax.rem(m, 4) + dx, 4)

    def xy_from(n):
        dy, dx = bend(n // 4), bend(lax.rem(n, 4))
        return lax.rem(m // 4 + 4 - dy, 4) * 4 + lax.rem(lax.rem(m, 4) + 4 - dx, 4)

    def far(n):
        odd = lax.rem(n, 2)
        return 8 + (1 - odd) * (n // 2) - odd * ((n + 1) // 2)

    def z_to(n):
        return lax.rem(z + far(n), NZ)

    def z_from(n):
        return lax.rem(z + NZ - far(n), NZ)

    x_up = (lax.rem(gx + 1, GX), gy)
    x_down = (lax.rem(gx + GX - 1, GX), gy)
    y_up = (gx, lax.rem(gy + 1, GY))
    y_down = (gx, lax.rem(gy + GY - 1, GY))

    def rcopy(src, dst, ssem, rsem, dev):
        return pltpu.make_async_remote_copy(
            src_ref=src, dst_ref=dst, send_sem=ssem, recv_sem=rsem,
            device_id=dev, device_id_type=pl.DeviceIdType.MESH,
        )

    barrier = pltpu.get_barrier_semaphore()

    def greet(dev):
        pl.semaphore_signal(barrier, inc=1, device_id=dev, device_id_type=pl.DeviceIdType.MESH)

    def greet_ring(i, carry):
        greet(z_dev(z_to(i)))
        greet(xy_dev(xy_to(i)))
        return carry

    lax.fori_loop(0, XY - 1, greet_ring, 0)
    greet(sib)
    for dev in (x_up, x_down, y_up, y_down):
        greet(dev)
    for n in later_loads:
        loads[n].start()

    loads[1].wait()
    x3 = pos[...]
    xhi = x3.astype(bf16).astype(f32)
    xmid = (x3 - xhi).astype(bf16).astype(f32)
    xlo = (x3 - xhi) - xmid
    scr2[...] = jnp.zeros_like(scr2)
    scr2[0:3, :] = xhi
    scr2[8:11, :] = xmid
    scr2[16:19, :] = xlo
    xt_s[...] = scr2[...].T.astype(bf16)
    for n in (2, 0, 4):
        loads[n].wait()
    features = feat[...]
    charges_t = dot_nt(wch[...], features).astype(bf16).astype(f32)
    row_id = lax.broadcasted_iota(jnp.int32, (32, ATOMS), 0)
    qf_s[...] = charges_t
    padded = jnp.concatenate([charges_t, jnp.zeros((C, ATOMS), f32)], axis=0)
    qe_s[...] = jnp.where(row_id == C, 1.0, padded).astype(bf16)
    own_sum = jnp.broadcast_to(jnp.sum(charges_t, axis=1, keepdims=True), (C, 128))
    QS[0] = own_sum
    mean_s[...] = jnp.concatenate([own_sum * (1.0 / ATOMS)] * KBS, axis=1)

    lane_iota = lax.broadcasted_iota(jnp.int32, (ATOMS, 32), 0)

    def pick(list_ref, d, base):
        scr[:, 0:32] = jnp.where(list_ref[d : d + 1, :] == lane_iota + base, 1.0, 0.0)
        return scr[...].T[0:32].astype(bf16)

    ghost = [
        rcopy(GS.at[0], TAB.at[pl.ds(128, 32)], g_s.at[0], g_r.at[0], x_up),
        rcopy(GS.at[1], TAB.at[pl.ds(160, 32)], g_s.at[1], g_r.at[1], x_down),
        rcopy(GS.at[2], TAB.at[pl.ds(192, 32)], g_s.at[2], g_r.at[2], y_up),
        rcopy(GS.at[3], TAB.at[pl.ds(224, 32)], g_s.at[3], g_r.at[3], y_down),
    ]

    def qa_copy(i, slot):
        return rcopy(QS.at[0], QA.at[slot], qa_s, qa_r, xy_dev(i))

    qa_all = rcopy(QA.at[pl.ds(0, XY - 1)], QA.at[pl.ds(0, XY - 1)], qa_s, qa_r, sib)
    qc_copy = rcopy(QS.at[1], QC, qc_s, qc_r, sib)

    def qb_copy(i, slot):
        return rcopy(QS.at[2], QB.at[slot], qb_s, qb_r, z_dev(i))

    qb_all = rcopy(QB.at[pl.ds(0, NZ - 1)], QB.at[pl.ds(0, NZ - 1)], qb_s, qb_r, sib)

    def start_qa(n, carry):
        qa_copy(xy_to(n), m).start()
        return carry

    def sum_plane():
        qa_all.wait_recv()
        QA[m] = QS[0]
        total = QA[0]
        for j in range(1, XY):
            total = total + QA[j]
        QS[1] = total
        qc_copy.start()

    def sum_cores():
        qc_copy.wait_recv()
        QS[2] = QS[1] + QC[...]

        def start(n, carry):
            qb_copy(z_to(n), z).start()
            return carry

        lax.fori_loop(0, NZ - 1, start, 0)

    def piece_of(n):
        half = jnp.where(n < XY, 1 - h, h)
        return half * XY + xy_to(lax.rem(n, XY))

    def phases(n, turns):
        first = pl.multiple_of(piece_of(n) * PIECE, PIECE)
        k3 = wv[:, pl.ds(first, PIECE)].astype(f32)
        k8 = jnp.concatenate([k3, jnp.zeros((5, PIECE), f32)], axis=0)
        kb = jnp.concatenate([k8, k8, k8, jnp.zeros((8, PIECE), f32)], axis=0).astype(bf16)
        turns[...] = dot(xt_s[:, 0:32], kb)

    def waves(n, turns, recent):
        g = piece_of(n)
        for j in range(PIECE // 128):
            lanes = slice(j * 128, (j + 1) * 128)
            for p, wave in enumerate(cos_sin_turns(turns[:, lanes])):
                wave = wave.astype(bf16)
                W[g, p, :, lanes] = wave
                recent[p, :, lanes] = wave

    def meet(recent):
        return [dot(qe_s[...], recent[p])[0:RAW] for p in range(2)]

    def core_copy(i):
        return rcopy(CS.at[i], CR.at[i], c_s, c_r.at[i], sib)

    core_all = rcopy(CS, CR, c_s, c_r.at[0], sib)

    def keep_core(n, raw):
        i = xy_to(n)
        CS[i, 0] = raw[0]
        CS[i, 1] = raw[1]

    def xy_copy(i, slot):
        return rcopy(XS.at[i], XR.at[slot], x_s, x_r, xy_dev(i))

    xy_all = rcopy(XR.at[pl.ds(0, XY - 1)], XR.at[pl.ds(0, XY - 1)], x_s, x_r, sib)

    def split_units(units):
        high = units.astype(bf16).astype(f32)
        return jnp.concatenate([high, units - high], axis=0)

    def put_terms(i, raw, keep):
        core_copy(i).wait_recv()
        offset = mean_s[...]
        units = []
        for p in range(2):
            total = raw[p] + CR[i, p]
            unit = total[C : C + 1]
            units.append(unit)
            terms = (total[0:C] - offset * unit).astype(bf16)
            for kb in range(KBS):
                keep[2 * kb + p] = terms[:, kb * 128 : (kb + 1) * 128]
        split = split_units(jnp.concatenate(units, axis=0))
        keep[TILES] = jnp.concatenate(
            [split[:, kb * 128 : (kb + 1) * 128] for kb in range(KBS)], axis=0
        ).astype(bf16)

    def send_xy(n, raw):
        i = xy_to(lax.rem(n, XY))
        put_terms(i, raw, XS.at[i])
        xy_copy(i, m).start()

    def two_pieces(use):
        def body(step, carry):
            n = 2 * step + 1
            phases(n + 1, TA)
            raw = meet(WA)
            waves(n, TB, WB)
            use(n - 1, raw)
            phases(n + 2, TB)
            raw = meet(WB)
            waves(n + 1, TA, WA)
            use(n, raw)
            return carry

        return body

    phases(0, TA)
    phases(1, TB)
    waves(0, TA, WA)
    lax.fori_loop(0, 8, two_pieces(keep_core), 0)

    pl.semaphore_wait(barrier, 5 + 2 * (XY - 1))

    def start_core(n, carry):
        core_copy(xy_to(n)).start()
        return carry

    lax.fori_loop(0, XY - 1, start_qa, 0)
    lax.fori_loop(0, XY, start_core, 0)

    lax.fori_loop(8, 13, two_pieces(send_xy), 0)
    sum_plane()
    lax.fori_loop(13, 15, two_pieces(send_xy), 0)
    raw = meet(WA)
    waves(31, TB, WB)
    send_xy(30, raw)
    put_terms(m, meet(WB), XR.at[m])
    sum_cores()

    for n in later_loads:
        loads[n].wait()
    scr[...] = jnp.zeros_like(scr)
    TAB[0:ATOMS] = features
    for d in range(2):
        GS[d] = dot(pick(sx, d, 0), features).astype(bf16)
    ghost[0].start()
    ghost[1].start()

    scr2[...] = jnp.zeros_like(scr2)
    scr2[0:20, :] = win[...].astype(f32)
    wint_s[...] = scr2[...].T.astype(bf16)
    woutt_s[...] = wout[...].astype(f32).T.astype(bf16)
    gt_s[:, 0:128] = features.astype(f32).T.astype(bf16)
    slot_id = lax.broadcasted_iota(jnp.int32, (SLOTS, ATOMS), 0)
    swing, _ = cos_sin_turns(dist[...] * 0.1)
    env_s[...] = jnp.where(slot_id < cnt[...], 0.5 * (swing + 1.0), 0.0)

    centre = lax.broadcasted_iota(jnp.int32, (32, ATOMS), 0).astype(f32) * (5.0 / 19.0)
    table_row = lax.broadcasted_iota(jnp.int32, (2 * ATOMS, ATOMS), 0)
    sharpness = 0.02 * 19.0 * 19.0

    def message_step(i, running):
        base = i * GROUP
        basis, hot = [], []
        for u in range(GROUP):
            offset = dist[pl.ds(base + u, 1), :] - centre
            basis.append(jnp.exp(-sharpness * offset * offset).astype(bf16))
            hot.append(jnp.where(nbr[pl.ds(base + u, 1), :] == table_row, 1.0, 0.0).astype(bf16))
        for u in range(0, GROUP, 4):
            pre = dot(wint_s[:, 0:32], jnp.concatenate(basis[u : u + 4], axis=1))
            hidden = jnp.log(0.5 * jnp.exp(pre) + 0.5).astype(bf16)
            filters = dot(woutt_s[...], hidden)
            rows = dot(gt_s[...], jnp.concatenate(hot[u : u + 4], axis=1))
            both = filters * rows
            for v in range(4):
                running = running + env_s[pl.ds(base + u + v, 1), :] * both[:, v * 128 : (v + 1) * 128]
        return running

    ghost[0].wait_recv()
    ghost[1].wait_recv()
    scr[...] = jnp.zeros_like(scr)
    for d in range(2):
        rows = dot(pick(sy, d, 0), TAB[0:128]) + dot(pick(sy, d, 128)[:, 0:64], TAB[128:192])
        GS[2 + d] = rows.astype(bf16)
    ghost[2].start()
    ghost[3].start()

    xy_all.wait_recv()
    plane_mean = QS[2] * (1.0 / (2 * XY * ATOMS))
    for kb in range(KBS):
        totals = [jnp.zeros((C, 128), f32), jnp.zeros((C, 128), f32)]
        units = jnp.zeros((2, 128), f32)
        for j in range(XY):
            shift = QA[j] * (1.0 / ATOMS) - plane_mean
            parts = XR[j, TILES].astype(f32)
            unit = parts[4 * kb : 4 * kb + 2] + parts[4 * kb + 2 : 4 * kb + 4]
            units = units + unit
            for p in range(2):
                totals[p] = totals[p] + (
                    XR[j, 2 * kb + p].astype(f32) + shift * unit[p : p + 1]
                )
        ZS[kb, 0] = totals[0].astype(bf16)
        ZS[kb, 1] = totals[1].astype(bf16)
        ZS[kb, 2] = jnp.concatenate(
            [split_units(units), jnp.zeros((C - 4, 128), f32)], axis=0
        ).astype(bf16)

    def z_copy(i, slot):
        return rcopy(ZS.at[lax.rem(i, KBS)], ZR.at[slot], z_s, z_r, z_dev(i))

    z_all = rcopy(ZR.at[pl.ds(0, NZ - 1)], ZR.at[pl.ds(0, NZ - 1)], z_s, z_r, sib)

    def start_z(n, carry):
        z_copy(z_to(n), z).start()
        return carry

    lax.fori_loop(0, NZ - 1, start_z, 0)
    block = lax.rem(z, KBS)
    ZR[z] = ZS[block]
    QB[z] = QS[2]

    g_own = h * XY + m
    k_block = pl.multiple_of(g_own * PIECE + block * 128, 128)
    kt = wv[:, pl.ds(k_block, 128)].astype(f32)
    q2 = (TWO_PI * TWO_PI) * (
        kt[0:1] * kt[0:1] + kt[1:2] * kt[1:2] + 0.25 * (kt[2:3] * kt[2:3])
    )
    eye = lax.broadcasted_iota(jnp.int32, (C, C), 0) == lax.broadcasted_iota(jnp.int32, (C, C), 1)
    width = jnp.sum(jnp.where(eye, jnp.broadcast_to(fw[...], (C, C)), 0.0), axis=1, keepdims=True)
    wgt_s[...] = jnp.exp(-0.5 * (width * width) * q2) * ((TWO_PI * TWO_PI) / q2)

    ghost[2].wait_recv()
    ghost[3].wait_recv()
    gt_s[:, 128:256] = TAB[128:256].astype(f32).T.astype(bf16)
    messages = lax.fori_loop(0, SLOTS // GROUP, message_step, jnp.zeros((128, ATOMS), f32))
    message_rows = messages.astype(bf16).astype(f32).T.astype(bf16)
    base_s[...] = features.astype(f32) + dot(message_rows, wup[...])
    scr[...] = jnp.zeros_like(scr)
    scr2[...] = jnp.zeros_like(scr2)
    scr2[0:C, :] = wlong[...]

    qb_all.wait_recv()
    mean = QB[0]
    for j in range(1, NZ):
        mean = mean + QB[j]
    mean = mean * (1.0 / (GX * GY * ATOMS))
    QS[3] = mean

    qa_all.wait_send()
    qb_all.wait_send()
    qc_copy.wait_send()
    core_all.wait_send()
    xy_all.wait_send()
    for copy in ghost:
        copy.wait_send()

    z_all.wait_recv()
    totals = [jnp.zeros((C, 128), f32), jnp.zeros((C, 128), f32)]
    for j in range(NZ):
        shift = QB[j] * (1.0 / (2 * XY * ATOMS)) - mean
        parts = ZR[j, 2].astype(f32)
        for p in range(2):
            unit = parts[p : p + 1] + parts[2 + p : 3 + p]
            totals[p] = totals[p] + (ZR[j, p].astype(f32) + shift * unit)
    for p in range(2):
        FALL[g_own, block, p] = (totals[p] * wgt_s[...]).astype(bf16)

    def f_copy(delta, kb, slot):
        return rcopy(
            FALL.at[g_own, kb], FALL.at[g_own, kb], f_s.at[slot], f_r.at[kb],
            z_dev(wrap(z + delta)),
        )

    for n, delta in enumerate((2, 1, -1)):
        f_copy(delta, block, n).start()

    def block_of(turn):
        return lax.rem(block + turn + turn // 2 - 2 * (turn // 3), KBS)

    def a_copy(n, turn):
        kb = block_of(turn)
        return rcopy(
            FALL.at[g_own, kb], FALL.at[g_own, kb], a_s, a_r.at[turn * 4 + n // 4],
            xy_dev(xy_to(n)),
        )

    def b_copy(j, turn, group):
        kb = block_of(turn)
        return rcopy(
            FALL.at[h * XY + j, kb], FALL.at[h * XY + j, kb], b_s,
            b_r.at[turn * 4 + group], sib,
        )

    def send_block(turn):
        def start(n, carry):
            a_copy(n, turn).start()
            return carry

        lax.fori_loop(0, XY - 1, start, 0)
        b_copy(m, turn, 3).start()

    send_block(0)
    for turn in range(1, KBS):
        f_copy(1, block_of(turn), 0).wait_recv()
        send_block(turn)
    z_all.wait_send()
    for n in range(3):
        f_copy(1, block, n).wait_send()

    def project(half, group, turn, running):
        kb = block_of(turn)
        f0, f1, kf, w0, w1 = [], [], [], [], []
        for u in range(4):
            g = half * XY + xy_from(group * 4 + u)
            lanes = pl.ds(pl.multiple_of(kb * 128, 128), 128)
            f0.append(FALL[g, kb, 0])
            f1.append(FALL[g, kb, 1])
            kf.append(wv[:, pl.ds(pl.multiple_of(g * PIECE + kb * 128, 128), 128)])
            w0.append(W[g, 0, :, lanes])
            w1.append(W[g, 1, :, lanes])
        f0, f1, kf, w0, w1 = [jnp.concatenate(v, axis=1) for v in (f0, f1, kf, w0, w1)]
        kf = kf.astype(f32) * TWO_PI
        f0w, f1w = f0.astype(f32), f1.astype(f32)
        first, second = [f0], [f1]
        for d in range(3):
            first.append((kf[d : d + 1] * f1w).astype(bf16))
            second.append((-kf[d : d + 1] * f0w).astype(bf16))
        running = running + dot_nt(jnp.concatenate(first, axis=0), w0)
        return running + dot_nt(jnp.concatenate(second, axis=0), w1)

    def wait_near(step):
        turn, group = step // 4, lax.rem(step, 4)
        sem = a_r.at[step]

        @pl.when(group < 3)
        def _():
            rcopy(FALL.at[0], FALL.at[0], a_s, sem, sib).wait_recv()

        @pl.when(group == 3)
        def _():
            part = FALL.at[0, pl.ds(0, 3)]
            rcopy(part, part, a_s, sem, sib).wait_recv()

        for u in range(3):
            b_copy(xy_from(group * 4 + u), turn, group).start()

        @pl.when(group < 3)
        def _():
            b_copy(xy_from(group * 4 + 3), turn, group).start()

    def wait_other(step):
        rcopy(FALL.at[0], FALL.at[0], b_s, b_r.at[step], sib).wait_recv()

    def near(step, running):
        wait_near(step)
        return project(h, lax.rem(step, 4), step // 4, running)

    def other(step, running):
        wait_other(step)
        return project(1 - h, lax.rem(step, 4), step // 4, running)

    def both(step, running):
        wait_near(step)
        wait_other(step - LAG)
        running = project(h, lax.rem(step, 4), step // 4, running)
        return project(1 - h, lax.rem(step - LAG, 4), (step - LAG) // 4, running)

    fields = lax.fori_loop(0, LAG, near, jnp.zeros((4 * C, ATOMS), f32))
    fields = lax.fori_loop(LAG, 4 * KBS, both, fields)
    fields = lax.fori_loop(4 * KBS - LAG, 4 * KBS, other, fields)
    fields = fields * (1.0 / math.sqrt(GX * GY * ATOMS))

    centred = qf_s[...] - QS[3]
    for d in range(3):
        part = fields[(d + 1) * C : (d + 2) * C]
        frc_o[d : d + 1, :] = -FORCE_UNIT * jnp.sum(centred * part, axis=0, keepdims=True)
    scr[0:C, :] = fields[0:C]
    long_part = dot(scr[...].T, scr2[...], precision=lax.Precision.HIGHEST)
    upd_o[...] = (base_s[...] + long_part).astype(bf16)

    rest_a = FALL.at[pl.ds(0, XY - 1)]
    rcopy(rest_a, rest_a, a_s, a_r.at[0], sib).wait_send()
    rest_b = FALL.at[pl.ds(0, XY)]
    rcopy(rest_b, rest_b, b_s, b_r.at[0], sib).wait_send()


def per_device(*args):
    feat, pos, wv, fw, wch, win, wout, wup, wlong, sx, sy, nbr, cnt, dist = args
    operands = (
        feat, pos, wv, fw.reshape(1, C), wch.T, win, wout, wup, wlong, sx, sy, nbr,
        cnt.reshape(1, ATOMS), dist,
    )
    dma = pltpu.SemaphoreType.DMA
    scratch = [pltpu.VMEM(value.shape, value.dtype) for value in operands] + [
        pltpu.VMEM((PIECES, 2, ATOMS, PIECE), bf16),
        pltpu.VMEM((2, ATOMS, PIECE), bf16),
        pltpu.VMEM((2, ATOMS, PIECE), bf16),
        pltpu.VMEM((ATOMS, PIECE), f32),
        pltpu.VMEM((ATOMS, PIECE), f32),
        pltpu.VMEM((XY, 2, RAW, PIECE), f32),
        pltpu.VMEM((XY, 2, RAW, PIECE), f32),
        pltpu.VMEM((XY, TILES + 1, C, 128), bf16),
        pltpu.VMEM((XY, TILES + 1, C, 128), bf16),
        pltpu.VMEM((KBS, 3, C, 128), bf16),
        pltpu.VMEM((NZ, 3, C, 128), bf16),
        pltpu.VMEM((PIECES, KBS, 2, C, 128), bf16),
        pltpu.VMEM((4, C, 128), f32),
        pltpu.VMEM((XY, C, 128), f32),
        pltpu.VMEM((NZ, C, 128), f32),
        pltpu.VMEM((C, 128), f32),
        pltpu.VMEM((2 * ATOMS, 128), bf16),
        pltpu.VMEM((4, 32, 128), bf16),
        pltpu.VMEM((128, 128), f32),
        pltpu.VMEM((128, 128), f32),
        pltpu.VMEM((128, 128), f32),
        pltpu.VMEM((128, 128), bf16),
        pltpu.VMEM((32, ATOMS), bf16),
        pltpu.VMEM((C, ATOMS), f32),
        pltpu.VMEM((C, PIECE), f32),
        pltpu.VMEM((SLOTS, ATOMS), f32),
        pltpu.VMEM((C, 128), f32),
        pltpu.VMEM((128, 256), bf16),
        pltpu.VMEM((128, 128), bf16),
        pltpu.VMEM((128, 128), bf16),
        dma, dma, dma, dma, dma, dma,
        dma((4,)), dma((4,)),
        dma, dma((XY,)),
        dma, dma,
        dma, dma,
        dma((KBS,)), dma((KBS,)),
        dma, dma((4 * KBS,)),
        dma, dma((4 * KBS,)),
        dma((14,)),
    ]
    vmem = pl.BlockSpec(memory_space=pltpu.VMEM)
    return pl.pallas_call(
        kernel,
        out_shape=(
            jax.ShapeDtypeStruct((ATOMS, 128), bf16),
            jax.ShapeDtypeStruct((3, ATOMS), f32),
        ),
        in_specs=[pl.BlockSpec(memory_space=pl.ANY)] * 14,
        out_specs=(vmem, vmem),
        scratch_shapes=scratch,
        compiler_params=pltpu.CompilerParams(
            collective_id=0, has_side_effects=True, vmem_limit_bytes=56 * 1024 * 1024
        ),
    )(*operands)


def solution(mesh):
    atoms_first = P(("gx", "gy"), None)
    atoms_last = P(None, ("gx", "gy"))
    placed = (
        atoms_first, atoms_last, P(), P(), P(), P(), P(), P(), P(),
        atoms_last, atoms_last, atoms_last, P(("gx", "gy")), atoms_last,
    )
    return jax.shard_map(
        per_device,
        mesh=mesh,
        in_specs=placed,
        out_specs=(atoms_first, atoms_last),
        check_vma=False,
    )
```

```python
import functools
import math

import jax
import jax.numpy as jnp
from jax import lax
from jax.experimental import pallas as pl
from jax.experimental.pallas import tpu as pltpu
from jax.sharding import PartitionSpec as P

f32 = jnp.float32
bf16 = jnp.bfloat16

GX = 16
GY = 32
XY = 16
NZ = 16
ATOMS = 128
C = 16
K = 16384
PIECE = 512
PIECES = K // PIECE
TILES = 8
KBS = 4
SLOTS = 64
RAW = 24
GROUP = 8
CHIPS = 8
STEPS = KBS * XY // CHIPS

TWO_PI = 2.0 * math.pi
FORCE_UNIT = 0.001
MAGIC = 12582912.0

SIN_POLY = (-0.79116057, 3.59775961, -7.30781532, 4.44287955)
COS_POLY = (-1.72807912, 5.7151373, -6.97763258, 1.41420395)


def horner(u, poly):
    value = poly[0] * u + poly[1]
    for term in poly[2:]:
        value = value * u + term
    return value


def cos_sin_turns(turns):
    r = turns - ((turns + MAGIC) - MAGIC)
    u = r * r
    s = r * horner(u, SIN_POLY)
    c = horner(u, COS_POLY)
    return 1.0 - s * s, s * c


def dot(a, b, **kw):
    return jnp.dot(a, b, preferred_element_type=f32, **kw)


def dot_nt(a, b):
    return lax.dot_general(a, b, (((1,), (1,)), ((), ())), preferred_element_type=f32)


def kernel(*refs):
    sources, (upd_o, frc_o), held, rest = refs[:14], refs[14:16], refs[16:30], refs[30:]
    feat, pos, wv, fw, wch, win, wout, wup, wlong, sx, sy, nbr, cnt, dist = held
    (W, WA, WB, TA, TB, CS, CR, XS, XR, ZS, ZR, FALL, QS, QA, QB, QC, TAB, GS,
    scr, scr2, base_s, xt_s, qe_s, qf_s, mean_s, env_s, wgt_s, gt_s, wint_s, woutt_s,
    qa_s, qa_r, qb_s, qb_r, qc_s, qc_r, g_s, g_r, c_s, c_r, x_s, x_r, z_s, z_r, f_s, f_r,
    a_s, a_r, b_s, b_r, in_sem) = rest
    loads = [
        pltpu.make_async_copy(sources[n], held[n], in_sem.at[n]) for n in range(14)
    ]
    first_loads = (1, 2, 0, 4)
    later_loads = [n for n in range(14) if n not in first_loads]
    for n in first_loads:
        loads[n].start()
    gx = lax.axis_index("gx")
    gy = lax.axis_index("gy")
    h = lax.rem(gx, 2)
    z = gy // 2
    row, column, xl = gx // 4, lax.rem(gx // 2, 2) * 2 + lax.rem(gy, 2), lax.rem(gy, 2)
    m = row * 4 + column
    sib = (gx + 1 - 2 * h, gy)

    def wrap(i, size):
        return jnp.where(i >= size, i - size, i)

    rows_to = [wrap(row + d, 4) for d in range(4)]
    rows_from = [rows_to[(4 - d) % 4] for d in range(4)]
    columns_to = [wrap(column + d, 4) for d in range(4)]
    columns_from = [columns_to[(4 - d) % 4] for d in range(4)]
    high = [jnp.where(c >= 2, 1, 0) for c in columns_to]
    device_x = [2 * high[d] + h for d in range(4)]
    device_y = [2 * z + columns_to[d] - 2 * high[d] for d in range(4)]
    far_first = (2, 3, 1, 0)

    def xy_to(n):
        if isinstance(n, int):
            return rows_to[far_first[n // 4]] * 4 + columns_to[far_first[n % 4]]
        quarter = jnp.where(n >= 4, 1, 0) + jnp.where(n >= 8, 1, 0) + jnp.where(n >= 12, 1, 0)
        rest = n - 4 * quarter
        dy = jnp.where(quarter < 2, quarter + 2, 3 - quarter)
        dx = jnp.where(rest < 2, rest + 2, 3 - rest)
        return wrap(row + dy, 4) * 4 + wrap(column + dx, 4)

    def xy_from(n):
        return rows_from[far_first[n // 4]] * 4 + columns_from[far_first[n % 4]]

    def xy_dev(n):
        dy, dx = far_first[n // 4], far_first[n % 4]
        return (rows_to[dy] * 4 + device_x[dx], device_y[dx])

    z_far = (8, 7, 9, 6, 10, 5, 11, 4, 12, 3, 13, 2, 14, 1, 15)
    block = lax.rem(z, KBS)

    def z_dev(d):
        return (gx, 2 * wrap(z + d, NZ) + xl)

    x_up = (lax.rem(gx + 1, GX), gy)
    x_down = (lax.rem(gx + GX - 1, GX), gy)
    y_up = (gx, lax.rem(gy + 1, GY))
    y_down = (gx, lax.rem(gy + GY - 1, GY))

    def rcopy(src, dst, ssem, rsem, dev):
        return pltpu.make_async_remote_copy(
            src_ref=src, dst_ref=dst, send_sem=ssem, recv_sem=rsem,
            device_id=dev, device_id_type=pl.DeviceIdType.MESH,
        )

    barrier = pltpu.get_barrier_semaphore()

    def greet(dev):
        pl.semaphore_signal(barrier, inc=1, device_id=dev, device_id_type=pl.DeviceIdType.MESH)

    for n in range(XY - 1):
        greet(z_dev(z_far[n]))
        greet(xy_dev(n))
    greet(sib)
    for dev in (x_up, x_down, y_up, y_down):
        greet(dev)
    for n in later_loads:
        loads[n].start()

    loads[1].wait()
    x3 = pos[...]
    xhi = x3.astype(bf16).astype(f32)
    xmid = (x3 - xhi).astype(bf16).astype(f32)
    xlo = (x3 - xhi) - xmid
    scr2[...] = jnp.zeros_like(scr2)
    scr2[0:3, :] = xhi
    scr2[8:11, :] = xmid
    scr2[16:19, :] = xlo
    xt_s[...] = scr2[...].T.astype(bf16)
    for n in (2, 0, 4):
        loads[n].wait()
    features = feat[...]
    charges_t = dot_nt(wch[...], features).astype(bf16).astype(f32)
    row_id = lax.broadcasted_iota(jnp.int32, (32, ATOMS), 0)
    qf_s[...] = charges_t
    padded = jnp.concatenate([charges_t, jnp.zeros((C, ATOMS), f32)], axis=0)
    qe_s[...] = jnp.where(row_id == C, 1.0, padded).astype(bf16)
    own_sum = jnp.broadcast_to(jnp.sum(charges_t, axis=1, keepdims=True), (C, 128))
    QS[0] = own_sum

    lane_iota = lax.broadcasted_iota(jnp.int32, (ATOMS, 32), 0)

    def pick(list_ref, d, base):
        scr[:, 0:32] = jnp.where(list_ref[d : d + 1, :] == lane_iota + base, 1.0, 0.0)
        return scr[...].T[0:32].astype(bf16)

    ghost = [
        rcopy(GS.at[0], TAB.at[pl.ds(128, 32)], g_s.at[0], g_r.at[0], x_up),
        rcopy(GS.at[1], TAB.at[pl.ds(160, 32)], g_s.at[1], g_r.at[1], x_down),
        rcopy(GS.at[2], TAB.at[pl.ds(192, 32)], g_s.at[2], g_r.at[2], y_up),
        rcopy(GS.at[3], TAB.at[pl.ds(224, 32)], g_s.at[3], g_r.at[3], y_down),
    ]

    qc_copy = rcopy(QS.at[0], QC, qc_s, qc_r, sib)

    def qa_copy(n):
        return rcopy(QS.at[1], QA.at[m], qa_s, qa_r, xy_dev(n))

    qa_all = rcopy(QA.at[pl.ds(0, XY - 1)], QA.at[pl.ds(0, XY - 1)], qa_s, qa_r, sib)

    def qb_copy(n):
        return rcopy(QS.at[2], QB.at[z], qb_s, qb_r, z_dev(z_far[n]))

    qb_all = rcopy(QB.at[pl.ds(0, NZ - 1)], QB.at[pl.ds(0, NZ - 1)], qb_s, qb_r, sib)

    def sum_pair():
        qc_copy.wait_recv()
        pair = QS[0] + QC[...]
        QS[1] = pair
        mean_s[...] = jnp.concatenate([pair * (1.0 / (2 * ATOMS))] * KBS, axis=1)

        for n in range(XY - 1):
            qa_copy(n).start()

    def sum_plane():
        qa_all.wait_recv()
        QA[m] = QS[1]
        total = QA[0]
        for j in range(1, XY):
            total = total + QA[j]
        QS[2] = total

        for n in range(NZ - 1):
            qb_copy(n).start()

    def piece_of(n):
        half = jnp.where(n < XY, 1 - h, h)
        return half * XY + xy_to(wrap(n, XY))

    def phases(n, turns):
        first = pl.multiple_of(piece_of(n) * PIECE, PIECE)
        k3 = wv[:, pl.ds(first, PIECE)].astype(f32)
        k8 = jnp.concatenate([k3, jnp.zeros((5, PIECE), f32)], axis=0)
        kb = jnp.concatenate([k8, k8, k8, jnp.zeros((8, PIECE), f32)], axis=0).astype(bf16)
        turns[...] = dot(xt_s[:, 0:32], kb)

    def waves(n, turns, recent):
        g = piece_of(n)
        for j in range(PIECE // 128):
            lanes = slice(j * 128, (j + 1) * 128)
            for p, wave in enumerate(cos_sin_turns(turns[:, lanes])):
                wave = wave.astype(bf16)
                W[g, p, :, lanes] = wave
                recent[p, :, lanes] = wave

    def meet(recent):
        return [dot(qe_s[...], recent[p])[0:RAW] for p in range(2)]

    def core_copy(i):
        return rcopy(CS.at[i], CR.at[i], c_s, c_r.at[i], sib)

    core_all = rcopy(CS, CR, c_s, c_r.at[0], sib)

    def keep_core(n, raw):
        i = xy_to(n)
        CS[i, 0] = raw[0]
        CS[i, 1] = raw[1]

    def xy_copy(i, dev):
        return rcopy(XS.at[i], XR.at[m], x_s, x_r, dev)

    xy_all = rcopy(XR.at[pl.ds(0, XY - 1)], XR.at[pl.ds(0, XY - 1)], x_s, x_r, sib)

    def split_units(units):
        high = units.astype(bf16).astype(f32)
        return jnp.concatenate([high, units - high], axis=0)

    def put_terms(i, raw, keep):
        core_copy(i).wait_recv()
        offset = mean_s[...]
        units = []
        for p in range(2):
            total = raw[p] + CR[i, p]
            unit = total[C : C + 1]
            units.append(unit)
            terms = (total[0:C] - offset * unit).astype(bf16)
            for kb in range(KBS):
                keep[2 * kb + p] = terms[:, kb * 128 : (kb + 1) * 128]
        split = split_units(jnp.concatenate(units, axis=0))
        keep[TILES] = jnp.concatenate(
            [split[:, kb * 128 : (kb + 1) * 128] for kb in range(KBS)], axis=0
        ).astype(bf16)

    def send_xy(n, raw):
        i = xy_to(wrap(n, XY))
        put_terms(i, raw, XS.at[i])
        y = jnp.where(i >= 4, 1, 0) + jnp.where(i >= 8, 1, 0) + jnp.where(i >= 12, 1, 0)
        x = i - 4 * y
        upper = jnp.where(x >= 2, 1, 0)
        xy_copy(i, (4 * y + 2 * upper + h, 2 * z + x - 2 * upper)).start()

    def two_pieces(use):
        def body(step, carry):
            n = 2 * step + 1
            phases(n + 1, TA)
            raw = meet(WA)
            waves(n, TB, WB)
            use(n - 1, raw)
            phases(n + 2, TB)
            raw = meet(WB)
            waves(n + 1, TA, WA)
            use(n, raw)
            return carry

        return body

    phases(0, TA)
    phases(1, TB)
    waves(0, TA, WA)
    lax.fori_loop(0, 8, two_pieces(keep_core), 0)

    pl.semaphore_wait(barrier, 5 + 2 * (XY - 1))

    def start_core(n, carry):
        core_copy(xy_to(n)).start()
        return carry

    qc_copy.start()
    lax.fori_loop(0, 4, start_core, 0)

    for n in later_loads:
        loads[n].wait()
    scr[...] = jnp.zeros_like(scr)
    TAB[0:ATOMS] = features
    for d in range(2):
        GS[d] = dot(pick(sx, d, 0), features).astype(bf16)
    ghost[0].start()
    ghost[1].start()

    sum_pair()
    lax.fori_loop(4, XY, start_core, 0)

    lax.fori_loop(8, 12, two_pieces(send_xy), 0)
    sum_plane()
    lax.fori_loop(12, 15, two_pieces(send_xy), 0)
    raw = meet(WA)
    waves(31, TB, WB)
    send_xy(30, raw)
    put_terms(m, meet(WB), XR.at[m])

    scr2[...] = jnp.zeros_like(scr2)
    scr2[0:20, :] = win[...].astype(f32)
    wint_s[...] = scr2[...].T.astype(bf16)
    woutt_s[...] = wout[...].astype(f32).T.astype(bf16)
    gt_s[:, 0:128] = features.astype(f32).T.astype(bf16)
    slot_id = lax.broadcasted_iota(jnp.int32, (SLOTS, ATOMS), 0)
    swing, _ = cos_sin_turns(dist[...] * 0.1)
    env_s[...] = jnp.where(slot_id < cnt[...], 0.5 * (swing + 1.0), 0.0)

    centre = lax.broadcasted_iota(jnp.int32, (32, ATOMS), 0).astype(f32) * (5.0 / 19.0)
    table_row = lax.broadcasted_iota(jnp.int32, (2 * ATOMS, ATOMS), 0)
    sharpness = 0.02 * 19.0 * 19.0

    def message_step(i, running):
        base = i * GROUP
        basis, hot = [], []
        for u in range(GROUP):
            offset = dist[pl.ds(base + u, 1), :] - centre
            basis.append(jnp.exp(-sharpness * offset * offset).astype(bf16))
            hot.append(jnp.where(nbr[pl.ds(base + u, 1), :] == table_row, 1.0, 0.0).astype(bf16))
        for u in range(0, GROUP, 4):
            pre = dot(wint_s[:, 0:32], jnp.concatenate(basis[u : u + 4], axis=1))
            hidden = jnp.log(0.5 * jnp.exp(pre) + 0.5).astype(bf16)
            filters = dot(woutt_s[...], hidden)
            rows = dot(gt_s[...], jnp.concatenate(hot[u : u + 4], axis=1))
            both = filters * rows
            for v in range(4):
                running = running + env_s[pl.ds(base + u + v, 1), :] * both[:, v * 128 : (v + 1) * 128]
        return running

    ghost[0].wait_recv()
    ghost[1].wait_recv()
    scr[...] = jnp.zeros_like(scr)
    for d in range(2):
        rows = dot(pick(sy, d, 0), TAB[0:128]) + dot(pick(sy, d, 128)[:, 0:64], TAB[128:192])
        GS[2 + d] = rows.astype(bf16)
    ghost[2].start()
    ghost[3].start()

    qb_all.wait_recv()
    QB[z] = QS[2]
    mean = QB[0]
    for j in range(1, NZ):
        mean = mean + QB[j]
    mean = mean * (1.0 / (GX * GY * ATOMS))
    QS[3] = mean
    xy_all.wait_recv()
    for kb in range(KBS):
        totals = [jnp.zeros((C, 128), f32), jnp.zeros((C, 128), f32)]
        for j in range(XY):
            shift = QA[j] * (1.0 / (2 * ATOMS)) - mean
            parts = XR[j, TILES].astype(f32)
            unit = parts[4 * kb : 4 * kb + 2] + parts[4 * kb + 2 : 4 * kb + 4]
            for p in range(2):
                totals[p] = totals[p] + (
                    XR[j, 2 * kb + p].astype(f32) + shift * unit[p : p + 1]
                )
        ZS[kb, 0] = totals[0].astype(bf16)
        ZS[kb, 1] = totals[1].astype(bf16)

    def z_copy(n):
        return rcopy(
            ZS.at[wrap(block + z_far[n] % KBS, KBS)], ZR.at[z], z_s, z_r, z_dev(z_far[n])
        )

    z_all = rcopy(ZR.at[pl.ds(0, NZ - 1)], ZR.at[pl.ds(0, NZ - 1)], z_s, z_r, sib)

    for n in range(NZ - 1):
        z_copy(n).start()
    ZR[z] = ZS[block]

    g_own = h * XY + m
    k_block = pl.multiple_of(g_own * PIECE + block * 128, 128)
    kt = wv[:, pl.ds(k_block, 128)].astype(f32)
    q2 = (TWO_PI * TWO_PI) * (
        kt[0:1] * kt[0:1] + kt[1:2] * kt[1:2] + 0.25 * (kt[2:3] * kt[2:3])
    )
    eye = lax.broadcasted_iota(jnp.int32, (C, C), 0) == lax.broadcasted_iota(jnp.int32, (C, C), 1)
    width = jnp.sum(jnp.where(eye, jnp.broadcast_to(fw[...], (C, C)), 0.0), axis=1, keepdims=True)
    wgt_s[...] = jnp.exp(-0.5 * (width * width) * q2) * ((TWO_PI * TWO_PI) / q2)

    ghost[2].wait_recv()
    ghost[3].wait_recv()
    gt_s[:, 128:256] = TAB[128:256].astype(f32).T.astype(bf16)
    messages = lax.fori_loop(0, SLOTS // GROUP, message_step, jnp.zeros((128, ATOMS), f32))
    message_rows = messages.astype(bf16).astype(f32).T.astype(bf16)
    base_s[...] = features.astype(f32) + dot(message_rows, wup[...])
    scr[...] = jnp.zeros_like(scr)
    scr2[...] = jnp.zeros_like(scr2)
    scr2[0:C, :] = wlong[...]

    qa_all.wait_send()
    qb_all.wait_send()
    qc_copy.wait_send()
    core_all.wait_send()
    xy_all.wait_send()
    for copy in ghost:
        copy.wait_send()

    z_all.wait_recv()
    totals = [jnp.zeros((C, 128), f32), jnp.zeros((C, 128), f32)]
    for j in range(NZ):
        for p in range(2):
            totals[p] = totals[p] + ZR[j, p].astype(f32)
    for p in range(2):
        FALL[g_own, block, p] = (totals[p] * wgt_s[...]).astype(bf16)

    def f_copy(delta, kb, slot):
        return rcopy(
            FALL.at[g_own, kb], FALL.at[g_own, kb], f_s.at[slot], f_r.at[kb],
            z_dev(delta % NZ),
        )

    for n, delta in enumerate((2, 1, -1)):
        f_copy(delta, block, n).start()

    def block_of(turn):
        if isinstance(turn, int):
            return wrap(block + (0, 1, 3, 2)[turn], KBS)
        return wrap(block + jnp.where(turn < 2, turn, 5 - turn), KBS)

    def a_copy(n, turn):
        kb = block_of(turn)
        return rcopy(
            FALL.at[g_own, kb], FALL.at[g_own, kb], a_s, a_r.at[turn * 2 + n // CHIPS],
            xy_dev(n),
        )

    def b_copy(j, turn, group):
        kb = block_of(turn)
        return rcopy(
            FALL.at[h * XY + j, kb], FALL.at[h * XY + j, kb], b_s,
            b_r.at[turn * 2 + group], sib,
        )

    def send_block(turn):
        for n in range(XY - 1):
            a_copy(n, turn).start()
        b_copy(m, turn, 1).start()

    send_block(0)
    for turn in range(1, KBS):
        f_copy(1, block_of(turn), 0).wait_recv()
        send_block(turn)
    z_all.wait_send()
    for n in range(3):
        f_copy(1, block, n).wait_send()

    def project(half, group, turn, running):
        kb = block_of(turn)
        f0, f1, kf, w0, w1 = [], [], [], [], []
        for u in range(CHIPS):
            g = half * XY + xy_from(group * CHIPS + u)
            lanes = pl.ds(pl.multiple_of(kb * 128, 128), 128)
            f0.append(FALL[g, kb, 0])
            f1.append(FALL[g, kb, 1])
            kf.append(wv[:, pl.ds(pl.multiple_of(g * PIECE + kb * 128, 128), 128)])
            w0.append(W[g, 0, :, lanes])
            w1.append(W[g, 1, :, lanes])
        f0, f1, kf, w0, w1 = [jnp.concatenate(v, axis=1) for v in (f0, f1, kf, w0, w1)]
        kf = kf.astype(f32) * TWO_PI
        f0w, f1w = f0.astype(f32), f1.astype(f32)
        first, second = [f0], [f1]
        for d in range(3):
            first.append((kf[d : d + 1] * f1w).astype(bf16))
            second.append((-kf[d : d + 1] * f0w).astype(bf16))
        running = running + dot_nt(w0, jnp.concatenate(first, axis=0))
        return running + dot_nt(w1, jnp.concatenate(second, axis=0))

    def wait_near(turn, group):
        chips = FALL.at[pl.ds(0, CHIPS - group), 0]
        rcopy(chips, chips, a_s, a_r.at[turn * 2 + group], sib).wait_recv()
        for u in range(CHIPS - group):
            b_copy(xy_from(group * CHIPS + u), turn, group).start()

    def wait_other(turn, group):
        chips = FALL.at[pl.ds(0, CHIPS), 0]
        rcopy(chips, chips, b_s, b_r.at[turn * 2 + group], sib).wait_recv()

    def first_turn(running):
        for group in range(2):
            wait_near(0, group)
            running = project(h, group, 0, running)
        return running

    def next_turn(turn, running):
        for group in range(2):
            wait_near(turn, group)
            wait_other(turn - 1, group)
            running = project(h, group, turn, running)
            running = project(1 - h, group, turn - 1, running)
        return running

    def last_turn(running):
        for group in range(2):
            wait_other(KBS - 1, group)
            running = project(1 - h, group, KBS - 1, running)
        return running

    fields = first_turn(jnp.zeros((ATOMS, 4 * C), f32))
    fields = lax.fori_loop(1, KBS, next_turn, fields)
    fields = last_turn(fields)

    scr[:, 0 : 4 * C] = fields * (1.0 / math.sqrt(GX * GY * ATOMS))
    columns = scr[...]
    long_part = dot(columns, scr2[...], precision=lax.Precision.HIGHEST)
    rows = columns.T
    centred = qf_s[...] - QS[3]
    for d in range(3):
        part = rows[(d + 1) * C : (d + 2) * C]
        frc_o[d : d + 1, :] = -FORCE_UNIT * jnp.sum(centred * part, axis=0, keepdims=True)
    upd_o[...] = (base_s[...] + long_part).astype(bf16)

    rest_a = FALL.at[pl.ds(0, XY - 1)]
    rcopy(rest_a, rest_a, a_s, a_r.at[0], sib).wait_send()
    rest_b = FALL.at[pl.ds(0, XY)]
    rcopy(rest_b, rest_b, b_s, b_r.at[0], sib).wait_send()


def per_device(*args):
    feat, pos, wv, fw, wch, win, wout, wup, wlong, sx, sy, nbr, cnt, dist = args
    operands = (
        feat, pos, wv, fw.reshape(1, C), wch.T, win, wout, wup, wlong, sx, sy, nbr,
        cnt.reshape(1, ATOMS), dist,
    )
    dma = pltpu.SemaphoreType.DMA
    scratch = [pltpu.VMEM(value.shape, value.dtype) for value in operands] + [
        pltpu.VMEM((PIECES, 2, ATOMS, PIECE), bf16),
        pltpu.VMEM((2, ATOMS, PIECE), bf16),
        pltpu.VMEM((2, ATOMS, PIECE), bf16),
        pltpu.VMEM((ATOMS, PIECE), f32),
        pltpu.VMEM((ATOMS, PIECE), f32),
        pltpu.VMEM((XY, 2, RAW, PIECE), f32),
        pltpu.VMEM((XY, 2, RAW, PIECE), f32),
        pltpu.VMEM((XY, TILES + 1, C, 128), bf16),
        pltpu.VMEM((XY, TILES + 1, C, 128), bf16),
        pltpu.VMEM((KBS, 2, C, 128), bf16),
        pltpu.VMEM((NZ, 2, C, 128), bf16),
        pltpu.VMEM((PIECES, KBS, 2, C, 128), bf16),
        pltpu.VMEM((4, C, 128), f32),
        pltpu.VMEM((XY, C, 128), f32),
        pltpu.VMEM((NZ, C, 128), f32),
        pltpu.VMEM((C, 128), f32),
        pltpu.VMEM((2 * ATOMS, 128), bf16),
        pltpu.VMEM((4, 32, 128), bf16),
        pltpu.VMEM((128, 128), f32),
        pltpu.VMEM((128, 128), f32),
        pltpu.VMEM((128, 128), f32),
        pltpu.VMEM((128, 128), bf16),
        pltpu.VMEM((32, ATOMS), bf16),
        pltpu.VMEM((C, ATOMS), f32),
        pltpu.VMEM((C, PIECE), f32),
        pltpu.VMEM((SLOTS, ATOMS), f32),
        pltpu.VMEM((C, 128), f32),
        pltpu.VMEM((128, 256), bf16),
        pltpu.VMEM((128, 128), bf16),
        pltpu.VMEM((128, 128), bf16),
        dma, dma, dma, dma, dma, dma,
        dma((4,)), dma((4,)),
        dma, dma((XY,)),
        dma, dma,
        dma, dma,
        dma((KBS,)), dma((KBS,)),
        dma, dma((STEPS,)),
        dma, dma((STEPS,)),
        dma((14,)),
    ]
    vmem = pl.BlockSpec(memory_space=pltpu.VMEM)
    return pl.pallas_call(
        kernel,
        out_shape=(
            jax.ShapeDtypeStruct((ATOMS, 128), bf16),
            jax.ShapeDtypeStruct((3, ATOMS), f32),
        ),
        in_specs=[pl.BlockSpec(memory_space=pl.ANY)] * 14,
        out_specs=(vmem, vmem),
        scratch_shapes=scratch,
        compiler_params=pltpu.CompilerParams(
            collective_id=0, has_side_effects=True, vmem_limit_bytes=56 * 1024 * 1024
        ),
    )(*operands)


def solution(mesh):
    atoms_first = P(("gx", "gy"), None)
    atoms_last = P(None, ("gx", "gy"))
    placed = (
        atoms_first, atoms_last, P(), P(), P(), P(), P(), P(), P(),
        atoms_last, atoms_last, atoms_last, P(("gx", "gy")), atoms_last,
    )
    return jax.shard_map(
        per_device,
        mesh=mesh,
        in_specs=placed,
        out_specs=(atoms_first, atoms_last),
        check_vma=False,
    )
```

```python
import functools
import math

import jax
import jax.numpy as jnp
from jax import lax
from jax.experimental import pallas as pl
from jax.experimental.pallas import tpu as pltpu
from jax.sharding import PartitionSpec as P

f32 = jnp.float32
bf16 = jnp.bfloat16

GX = 16
GY = 32
XY = 16
NZ = 16
ATOMS = 128
C = 16
K = 16384
PIECE = 512
PIECES = K // PIECE
TILES = 8
KBS = 4
SLOTS = 64
RAW = 24
GROUP = 8
CHIPS = 8
STEPS = KBS * XY // CHIPS

TWO_PI = 2.0 * math.pi
FORCE_UNIT = 0.001
MAGIC = 12582912.0

SIN_POLY = (-0.79116057, 3.59775961, -7.30781532, 4.44287955)
COS_POLY = (-1.72807912, 5.7151373, -6.97763258, 1.41420395)


def horner(u, poly):
    value = poly[0] * u + poly[1]
    for term in poly[2:]:
        value = value * u + term
    return value


def cos_sin_turns(turns):
    r = turns - ((turns + MAGIC) - MAGIC)
    u = r * r
    s = r * horner(u, SIN_POLY)
    c = horner(u, COS_POLY)
    return 1.0 - s * s, s * c


def dot(a, b, **kw):
    return jnp.dot(a, b, preferred_element_type=f32, **kw)


def dot_nt(a, b):
    return lax.dot_general(a, b, (((1,), (1,)), ((), ())), preferred_element_type=f32)


def kernel(*refs):
    sources, (upd_o, frc_o), held, rest = refs[:14], refs[14:16], refs[16:30], refs[30:]
    feat, pos, wv, fw, wch, win, wout, wup, wlong, sx, sy, nbr, cnt, dist = held
    (W, WA, WB, TA, TB, CS, CR, XS, XR, ZS, ZR, FALL, QS, QA, QB, QC, TAB, GS,
    scr, scr2, base_s, xt_s, qe_s, qf_s, mean_s, env_s, wgt_s, gt_s, wint_s, woutt_s,
    qa_s, qa_r, qb_s, qb_r, qc_s, qc_r, g_s, g_r, c_s, c_r, x_s, x_r, z_s, z_r, f_s, f_r,
    a_s, a_r, b_s, b_r, in_sem) = rest
    loads = [
        pltpu.make_async_copy(sources[n], held[n], in_sem.at[n]) for n in range(14)
    ]
    first_loads = (1, 2, 0, 4)
    later_loads = [n for n in range(14) if n not in first_loads]
    for n in first_loads:
        loads[n].start()
    gx = lax.axis_index("gx")
    gy = lax.axis_index("gy")
    h = lax.rem(gx, 2)
    z = gy // 2
    row, column, xl = gx // 4, lax.rem(gx // 2, 2) * 2 + lax.rem(gy, 2), lax.rem(gy, 2)
    m = row * 4 + column
    sib = (gx + 1 - 2 * h, gy)

    def wrap(i, size):
        return jnp.where(i >= size, i - size, i)

    rows_to = [wrap(row + d, 4) for d in range(4)]
    rows_from = [rows_to[(4 - d) % 4] for d in range(4)]
    columns_to = [wrap(column + d, 4) for d in range(4)]
    columns_from = [columns_to[(4 - d) % 4] for d in range(4)]
    high = [jnp.where(c >= 2, 1, 0) for c in columns_to]
    device_x = [2 * high[d] + h for d in range(4)]
    device_y = [2 * z + columns_to[d] - 2 * high[d] for d in range(4)]
    far_first = (2, 3, 1, 0)

    def xy_to(n):
        if isinstance(n, int):
            return rows_to[far_first[n // 4]] * 4 + columns_to[far_first[n % 4]]
        quarter = jnp.where(n >= 4, 1, 0) + jnp.where(n >= 8, 1, 0) + jnp.where(n >= 12, 1, 0)
        rest = n - 4 * quarter
        dy = jnp.where(quarter < 2, quarter + 2, 3 - quarter)
        dx = jnp.where(rest < 2, rest + 2, 3 - rest)
        return wrap(row + dy, 4) * 4 + wrap(column + dx, 4)

    def xy_from(n):
        return rows_from[far_first[n // 4]] * 4 + columns_from[far_first[n % 4]]

    def xy_dev(n):
        dy, dx = far_first[n // 4], far_first[n % 4]
        return (rows_to[dy] * 4 + device_x[dx], device_y[dx])

    z_far = (8, 7, 9, 6, 10, 5, 11, 4, 12, 3, 13, 2, 14, 1, 15)
    block = lax.rem(z, KBS)

    def z_dev(d):
        return (gx, 2 * wrap(z + d, NZ) + xl)

    x_up = (lax.rem(gx + 1, GX), gy)
    x_down = (lax.rem(gx + GX - 1, GX), gy)
    y_up = (gx, lax.rem(gy + 1, GY))
    y_down = (gx, lax.rem(gy + GY - 1, GY))

    def rcopy(src, dst, ssem, rsem, dev):
        return pltpu.make_async_remote_copy(
            src_ref=src, dst_ref=dst, send_sem=ssem, recv_sem=rsem,
            device_id=dev, device_id_type=pl.DeviceIdType.MESH,
        )

    barrier = pltpu.get_barrier_semaphore()

    def greet(dev):
        pl.semaphore_signal(barrier, inc=1, device_id=dev, device_id_type=pl.DeviceIdType.MESH)

    for n in range(XY - 1):
        greet(z_dev(z_far[n]))
        greet(xy_dev(n))
    greet(sib)
    for dev in (x_up, x_down, y_up, y_down):
        greet(dev)
    for n in later_loads:
        loads[n].start()

    loads[1].wait()
    x3 = pos[...]
    xhi = x3.astype(bf16).astype(f32)
    xmid = (x3 - xhi).astype(bf16).astype(f32)
    xlo = (x3 - xhi) - xmid
    scr2[...] = jnp.zeros_like(scr2)
    scr2[0:3, :] = xhi
    scr2[8:11, :] = xmid
    scr2[16:19, :] = xlo
    xt_s[...] = scr2[...].T.astype(bf16)
    for n in (2, 0, 4):
        loads[n].wait()
    features = feat[...]
    charges_t = dot_nt(wch[...], features).astype(bf16).astype(f32)
    row_id = lax.broadcasted_iota(jnp.int32, (32, ATOMS), 0)
    qf_s[...] = charges_t
    padded = jnp.concatenate([charges_t, jnp.zeros((C, ATOMS), f32)], axis=0)
    qe_s[...] = jnp.where(row_id == C, 1.0, padded).astype(bf16)
    own_sum = jnp.broadcast_to(jnp.sum(charges_t, axis=1, keepdims=True), (C, 128))
    QS[0] = own_sum

    lane_iota = lax.broadcasted_iota(jnp.int32, (ATOMS, 32), 0)

    def pick(list_ref, d, base):
        scr[:, 0:32] = jnp.where(list_ref[d : d + 1, :] == lane_iota + base, 1.0, 0.0)
        return scr[...].T[0:32].astype(bf16)

    ghost = [
        rcopy(GS.at[0], TAB.at[pl.ds(128, 32)], g_s.at[0], g_r.at[0], x_up),
        rcopy(GS.at[1], TAB.at[pl.ds(160, 32)], g_s.at[1], g_r.at[1], x_down),
        rcopy(GS.at[2], TAB.at[pl.ds(192, 32)], g_s.at[2], g_r.at[2], y_up),
        rcopy(GS.at[3], TAB.at[pl.ds(224, 32)], g_s.at[3], g_r.at[3], y_down),
    ]

    qc_copy = rcopy(QS.at[0], QC, qc_s, qc_r, sib)

    def qa_copy(n):
        return rcopy(QS.at[1], QA.at[m], qa_s, qa_r, xy_dev(n))

    qa_all = rcopy(QA.at[pl.ds(0, XY - 1)], QA.at[pl.ds(0, XY - 1)], qa_s, qa_r, sib)

    def qb_copy(n):
        return rcopy(QS.at[2], QB.at[z], qb_s, qb_r, z_dev(z_far[n]))

    qb_all = rcopy(QB.at[pl.ds(0, NZ - 1)], QB.at[pl.ds(0, NZ - 1)], qb_s, qb_r, sib)

    def sum_pair():
        qc_copy.wait_recv()
        pair = QS[0] + QC[...]
        QS[1] = pair
        mean_s[...] = jnp.concatenate([pair * (1.0 / (2 * ATOMS))] * KBS, axis=1)

        for n in range(XY - 1):
            qa_copy(n).start()

    def sum_plane():
        qa_all.wait_recv()
        QA[m] = QS[1]
        total = QA[0]
        for j in range(1, XY):
            total = total + QA[j]
        QS[2] = total

        for n in range(NZ - 1):
            qb_copy(n).start()

    def piece_of(n):
        half = jnp.where(n < XY, 1 - h, h)
        return half * XY + xy_to(wrap(n, XY))

    def phases(n, turns):
        first = pl.multiple_of(piece_of(n) * PIECE, PIECE)
        k3 = wv[:, pl.ds(first, PIECE)].astype(f32)
        k8 = jnp.concatenate([k3, jnp.zeros((5, PIECE), f32)], axis=0)
        kb = jnp.concatenate([k8, k8, k8, jnp.zeros((8, PIECE), f32)], axis=0).astype(bf16)
        turns[...] = dot(xt_s[:, 0:32], kb)

    def waves(n, turns, recent):
        g = piece_of(n)
        for j in range(PIECE // 128):
            lanes = slice(j * 128, (j + 1) * 128)
            for p, wave in enumerate(cos_sin_turns(turns[:, lanes])):
                wave = wave.astype(bf16)
                W[g, p, :, lanes] = wave
                recent[p, :, lanes] = wave

    def meet(recent):
        return [dot(qe_s[...], recent[p])[0:RAW] for p in range(2)]

    def core_copy(i):
        return rcopy(CS.at[i], CR.at[i], c_s, c_r.at[i], sib)

    core_all = rcopy(CS, CR, c_s, c_r.at[0], sib)

    def keep_core(n, raw):
        i = xy_to(n)
        CS[i, 0] = raw[0]
        CS[i, 1] = raw[1]

    def xy_copy(i, dev):
        return rcopy(XS.at[i], XR.at[m], x_s, x_r, dev)

    xy_all = rcopy(XR.at[pl.ds(0, XY - 1)], XR.at[pl.ds(0, XY - 1)], x_s, x_r, sib)

    def split_units(units):
        high = units.astype(bf16).astype(f32)
        return jnp.concatenate([high, units - high], axis=0)

    def put_terms(i, raw, keep):
        core_copy(i).wait_recv()
        offset = mean_s[...]
        units = []
        for p in range(2):
            total = raw[p] + CR[i, p]
            unit = total[C : C + 1]
            units.append(unit)
            terms = (total[0:C] - offset * unit).astype(bf16)
            for kb in range(KBS):
                keep[2 * kb + p] = terms[:, kb * 128 : (kb + 1) * 128]
        split = split_units(jnp.concatenate(units, axis=0))
        keep[TILES] = jnp.concatenate(
            [split[:, kb * 128 : (kb + 1) * 128] for kb in range(KBS)], axis=0
        ).astype(bf16)

    def send_xy(n, raw):
        i = xy_to(wrap(n, XY))
        put_terms(i, raw, XS.at[i])
        y = jnp.where(i >= 4, 1, 0) + jnp.where(i >= 8, 1, 0) + jnp.where(i >= 12, 1, 0)
        x = i - 4 * y
        upper = jnp.where(x >= 2, 1, 0)
        xy_copy(i, (4 * y + 2 * upper + h, 2 * z + x - 2 * upper)).start()

    def two_pieces(use):
        def body(step, carry):
            n = 2 * step + 1
            phases(n + 1, TA)
            raw = meet(WA)
            waves(n, TB, WB)
            use(n - 1, raw)
            phases(n + 2, TB)
            raw = meet(WB)
            waves(n + 1, TA, WA)
            use(n, raw)
            return carry

        return body

    phases(0, TA)
    phases(1, TB)
    waves(0, TA, WA)
    lax.fori_loop(0, 8, two_pieces(keep_core), 0)

    pl.semaphore_wait(barrier, 5 + 2 * (XY - 1))

    def start_core(n, carry):
        core_copy(xy_to(n)).start()
        return carry

    qc_copy.start()
    lax.fori_loop(0, 4, start_core, 0)

    for n in later_loads:
        loads[n].wait()
    scr[...] = jnp.zeros_like(scr)
    TAB[0:ATOMS] = features
    for d in range(2):
        GS[d] = dot(pick(sx, d, 0), features).astype(bf16)
    ghost[0].start()
    ghost[1].start()

    sum_pair()
    lax.fori_loop(4, XY, start_core, 0)

    send_two = two_pieces(send_xy)

    def own_half(step, carry):
        pl.when(step == 12)(sum_plane)
        return send_two(step, carry)

    lax.fori_loop(8, 15, own_half, 0)
    raw = meet(WA)
    waves(31, TB, WB)
    send_xy(30, raw)
    put_terms(m, meet(WB), XR.at[m])

    scr2[...] = jnp.zeros_like(scr2)
    scr2[0:20, :] = win[...].astype(f32)
    wint_s[...] = scr2[...].T.astype(bf16)
    woutt_s[...] = wout[...].astype(f32).T.astype(bf16)
    gt_s[:, 0:128] = features.astype(f32).T.astype(bf16)
    slot_id = lax.broadcasted_iota(jnp.int32, (SLOTS, ATOMS), 0)
    swing, _ = cos_sin_turns(dist[...] * 0.1)
    env_s[...] = jnp.where(slot_id < cnt[...], 0.5 * (swing + 1.0), 0.0)

    centre = lax.broadcasted_iota(jnp.int32, (32, ATOMS), 0).astype(f32) * (5.0 / 19.0)
    table_row = lax.broadcasted_iota(jnp.int32, (2 * ATOMS, ATOMS), 0)
    sharpness = 0.02 * 19.0 * 19.0

    def message_step(i, running):
        base = i * GROUP
        basis, hot = [], []
        for u in range(GROUP):
            offset = dist[pl.ds(base + u, 1), :] - centre
            basis.append(jnp.exp(-sharpness * offset * offset).astype(bf16))
            hot.append(jnp.where(nbr[pl.ds(base + u, 1), :] == table_row, 1.0, 0.0).astype(bf16))
        for u in range(0, GROUP, 4):
            pre = dot(wint_s[:, 0:32], jnp.concatenate(basis[u : u + 4], axis=1))
            hidden = jnp.log(0.5 * jnp.exp(pre) + 0.5).astype(bf16)
            filters = dot(woutt_s[...], hidden)
            rows = dot(gt_s[...], jnp.concatenate(hot[u : u + 4], axis=1))
            both = filters * rows
            for v in range(4):
                running = running + env_s[pl.ds(base + u + v, 1), :] * both[:, v * 128 : (v + 1) * 128]
        return running

    ghost[0].wait_recv()
    ghost[1].wait_recv()
    scr[...] = jnp.zeros_like(scr)
    for d in range(2):
        rows = dot(pick(sy, d, 0), TAB[0:128]) + dot(pick(sy, d, 128)[:, 0:64], TAB[128:192])
        GS[2 + d] = rows.astype(bf16)
    ghost[2].start()
    ghost[3].start()

    xy_all.wait_recv()
    pieces = []
    for kb in range(KBS):
        totals = [jnp.zeros((C, 128), f32), jnp.zeros((C, 128), f32)]
        units = jnp.zeros((2, 128), f32)
        for j in range(XY):
            parts = XR[j, TILES].astype(f32)
            unit = parts[4 * kb : 4 * kb + 2] + parts[4 * kb + 2 : 4 * kb + 4]
            units = units + unit
            offset = QA[j] * (1.0 / (2 * ATOMS))
            for p in range(2):
                totals[p] = totals[p] + (
                    XR[j, 2 * kb + p].astype(f32) + offset * unit[p : p + 1]
                )
        pieces.append((totals, units))
    qb_all.wait_recv()
    QB[z] = QS[2]
    mean = QB[0]
    for j in range(1, NZ):
        mean = mean + QB[j]
    mean = mean * (1.0 / (GX * GY * ATOMS))
    QS[3] = mean
    for kb, (totals, units) in enumerate(pieces):
        for p in range(2):
            ZS[kb, p] = (totals[p] - mean * units[p : p + 1]).astype(bf16)

    def z_copy(n):
        return rcopy(
            ZS.at[wrap(block + z_far[n] % KBS, KBS)], ZR.at[z], z_s, z_r, z_dev(z_far[n])
        )

    z_all = rcopy(ZR.at[pl.ds(0, NZ - 1)], ZR.at[pl.ds(0, NZ - 1)], z_s, z_r, sib)

    for n in range(NZ - 1):
        z_copy(n).start()
    ZR[z] = ZS[block]

    g_own = h * XY + m
    k_block = pl.multiple_of(g_own * PIECE + block * 128, 128)
    kt = wv[:, pl.ds(k_block, 128)].astype(f32)
    q2 = (TWO_PI * TWO_PI) * (
        kt[0:1] * kt[0:1] + kt[1:2] * kt[1:2] + 0.25 * (kt[2:3] * kt[2:3])
    )
    eye = lax.broadcasted_iota(jnp.int32, (C, C), 0) == lax.broadcasted_iota(jnp.int32, (C, C), 1)
    width = jnp.sum(jnp.where(eye, jnp.broadcast_to(fw[...], (C, C)), 0.0), axis=1, keepdims=True)
    wgt_s[...] = jnp.exp(-0.5 * (width * width) * q2) * ((TWO_PI * TWO_PI) / q2)

    ghost[2].wait_recv()
    ghost[3].wait_recv()
    gt_s[:, 128:256] = TAB[128:256].astype(f32).T.astype(bf16)
    messages = lax.fori_loop(0, SLOTS // GROUP, message_step, jnp.zeros((128, ATOMS), f32))
    message_rows = messages.astype(bf16).astype(f32).T.astype(bf16)
    base_s[...] = features.astype(f32) + dot(message_rows, wup[...])
    scr[...] = jnp.zeros_like(scr)
    scr2[...] = jnp.zeros_like(scr2)
    scr2[0:C, :] = wlong[...]

    qa_all.wait_send()
    qb_all.wait_send()
    qc_copy.wait_send()
    core_all.wait_send()
    xy_all.wait_send()
    for copy in ghost:
        copy.wait_send()

    z_all.wait_recv()
    totals = [jnp.zeros((C, 128), f32), jnp.zeros((C, 128), f32)]
    for j in range(NZ):
        for p in range(2):
            totals[p] = totals[p] + ZR[j, p].astype(f32)
    for p in range(2):
        FALL[g_own, block, p] = (totals[p] * wgt_s[...]).astype(bf16)

    def f_copy(delta, kb, slot):
        return rcopy(
            FALL.at[g_own, kb], FALL.at[g_own, kb], f_s.at[slot], f_r.at[kb],
            z_dev(delta % NZ),
        )

    for n, delta in enumerate((2, 1, -1)):
        f_copy(delta, block, n).start()

    def block_of(turn):
        if isinstance(turn, int):
            return wrap(block + (0, 1, 3, 2)[turn], KBS)
        return wrap(block + jnp.where(turn < 2, turn, 5 - turn), KBS)

    def a_copy(n, turn):
        kb = block_of(turn)
        return rcopy(
            FALL.at[g_own, kb], FALL.at[g_own, kb], a_s, a_r.at[turn * 2 + n // CHIPS],
            xy_dev(n),
        )

    def b_copy(j, turn, group):
        kb = block_of(turn)
        return rcopy(
            FALL.at[h * XY + j, kb], FALL.at[h * XY + j, kb], b_s,
            b_r.at[turn * 2 + group], sib,
        )

    def send_block(turn):
        for n in reversed(range(XY - 1)):
            a_copy(n, turn).start()
        b_copy(m, turn, 1).start()

    send_block(0)
    for turn in range(1, KBS):
        f_copy(1, block_of(turn), 0).wait_recv()
        send_block(turn)
    z_all.wait_send()
    for n in range(3):
        f_copy(1, block, n).wait_send()

    def project(half, group, turn, running):
        kb = block_of(turn)
        f0, f1, kf, w0, w1 = [], [], [], [], []
        for u in range(CHIPS):
            g = half * XY + xy_from(group * CHIPS + u)
            lanes = pl.ds(pl.multiple_of(kb * 128, 128), 128)
            f0.append(FALL[g, kb, 0])
            f1.append(FALL[g, kb, 1])
            kf.append(wv[:, pl.ds(pl.multiple_of(g * PIECE + kb * 128, 128), 128)])
            w0.append(W[g, 0, :, lanes])
            w1.append(W[g, 1, :, lanes])
        f0, f1, kf, w0, w1 = [jnp.concatenate(v, axis=1) for v in (f0, f1, kf, w0, w1)]
        kf = kf.astype(f32) * TWO_PI
        f0w, f1w = f0.astype(f32), f1.astype(f32)
        first, second = [f0], [f1]
        for d in range(3):
            first.append((kf[d : d + 1] * f1w).astype(bf16))
            second.append((-kf[d : d + 1] * f0w).astype(bf16))
        running = running + dot_nt(w0, jnp.concatenate(first, axis=0))
        return running + dot_nt(w1, jnp.concatenate(second, axis=0))

    def wait_near(turn, group):
        chips = FALL.at[pl.ds(0, CHIPS - group), 0]
        rcopy(chips, chips, a_s, a_r.at[turn * 2 + group], sib).wait_recv()
        for u in range(CHIPS - group):
            b_copy(xy_from(group * CHIPS + u), turn, group).start()

    def wait_other(turn, group):
        chips = FALL.at[pl.ds(0, CHIPS), 0]
        rcopy(chips, chips, b_s, b_r.at[turn * 2 + group], sib).wait_recv()

    def first_turn(running):
        for group in (1, 0):
            wait_near(0, group)
            running = project(h, group, 0, running)
        return running

    def next_turn(turn, running):
        for group in (1, 0):
            wait_near(turn, group)
            wait_other(turn - 1, group)
            running = project(h, group, turn, running)
            running = project(1 - h, group, turn - 1, running)
        return running

    def last_turn(running):
        for group in (1, 0):
            wait_other(KBS - 1, group)
            running = project(1 - h, group, KBS - 1, running)
        return running

    fields = first_turn(jnp.zeros((ATOMS, 4 * C), f32))
    fields = lax.fori_loop(1, KBS, next_turn, fields)
    fields = last_turn(fields)

    scr[:, 0 : 4 * C] = fields * (1.0 / math.sqrt(GX * GY * ATOMS))
    columns = scr[...]
    long_part = dot(columns, scr2[...], precision=lax.Precision.HIGHEST)
    rows = columns.T
    centred = qf_s[...] - QS[3]
    for d in range(3):
        part = rows[(d + 1) * C : (d + 2) * C]
        frc_o[d : d + 1, :] = -FORCE_UNIT * jnp.sum(centred * part, axis=0, keepdims=True)
    upd_o[...] = (base_s[...] + long_part).astype(bf16)

    rest_a = FALL.at[pl.ds(0, XY - 1)]
    rcopy(rest_a, rest_a, a_s, a_r.at[0], sib).wait_send()
    rest_b = FALL.at[pl.ds(0, XY)]
    rcopy(rest_b, rest_b, b_s, b_r.at[0], sib).wait_send()


def per_device(*args):
    feat, pos, wv, fw, wch, win, wout, wup, wlong, sx, sy, nbr, cnt, dist = args
    operands = (
        feat, pos, wv, fw.reshape(1, C), wch.T, win, wout, wup, wlong, sx, sy, nbr,
        cnt.reshape(1, ATOMS), dist,
    )
    dma = pltpu.SemaphoreType.DMA
    scratch = [pltpu.VMEM(value.shape, value.dtype) for value in operands] + [
        pltpu.VMEM((PIECES, 2, ATOMS, PIECE), bf16),
        pltpu.VMEM((2, ATOMS, PIECE), bf16),
        pltpu.VMEM((2, ATOMS, PIECE), bf16),
        pltpu.VMEM((ATOMS, PIECE), f32),
        pltpu.VMEM((ATOMS, PIECE), f32),
        pltpu.VMEM((XY, 2, RAW, PIECE), f32),
        pltpu.VMEM((XY, 2, RAW, PIECE), f32),
        pltpu.VMEM((XY, TILES + 1, C, 128), bf16),
        pltpu.VMEM((XY, TILES + 1, C, 128), bf16),
        pltpu.VMEM((KBS, 2, C, 128), bf16),
        pltpu.VMEM((NZ, 2, C, 128), bf16),
        pltpu.VMEM((PIECES, KBS, 2, C, 128), bf16),
        pltpu.VMEM((4, C, 128), f32),
        pltpu.VMEM((XY, C, 128), f32),
        pltpu.VMEM((NZ, C, 128), f32),
        pltpu.VMEM((C, 128), f32),
        pltpu.VMEM((2 * ATOMS, 128), bf16),
        pltpu.VMEM((4, 32, 128), bf16),
        pltpu.VMEM((128, 128), f32),
        pltpu.VMEM((128, 128), f32),
        pltpu.VMEM((128, 128), f32),
        pltpu.VMEM((128, 128), bf16),
        pltpu.VMEM((32, ATOMS), bf16),
        pltpu.VMEM((C, ATOMS), f32),
        pltpu.VMEM((C, PIECE), f32),
        pltpu.VMEM((SLOTS, ATOMS), f32),
        pltpu.VMEM((C, 128), f32),
        pltpu.VMEM((128, 256), bf16),
        pltpu.VMEM((128, 128), bf16),
        pltpu.VMEM((128, 128), bf16),
        dma, dma, dma, dma, dma, dma,
        dma((4,)), dma((4,)),
        dma, dma((XY,)),
        dma, dma,
        dma, dma,
        dma((KBS,)), dma((KBS,)),
        dma, dma((STEPS,)),
        dma, dma((STEPS,)),
        dma((14,)),
    ]
    vmem = pl.BlockSpec(memory_space=pltpu.VMEM)
    return pl.pallas_call(
        kernel,
        out_shape=(
            jax.ShapeDtypeStruct((ATOMS, 128), bf16),
            jax.ShapeDtypeStruct((3, ATOMS), f32),
        ),
        in_specs=[pl.BlockSpec(memory_space=pl.ANY)] * 14,
        out_specs=(vmem, vmem),
        scratch_shapes=scratch,
        compiler_params=pltpu.CompilerParams(
            collective_id=0, has_side_effects=True, vmem_limit_bytes=56 * 1024 * 1024
        ),
    )(*operands)


def solution(mesh):
    atoms_first = P(("gx", "gy"), None)
    atoms_last = P(None, ("gx", "gy"))
    placed = (
        atoms_first, atoms_last, P(), P(), P(), P(), P(), P(), P(),
        atoms_last, atoms_last, atoms_last, P(("gx", "gy")), atoms_last,
    )
    return jax.shard_map(
        per_device,
        mesh=mesh,
        in_specs=placed,
        out_specs=(atoms_first, atoms_last),
        check_vma=False,
    )
```

```python
import functools
import math

import jax
import jax.numpy as jnp
from jax import lax
from jax.experimental import pallas as pl
from jax.experimental.pallas import tpu as pltpu
from jax.sharding import PartitionSpec as P

f32 = jnp.float32
bf16 = jnp.bfloat16

GX = 16
GY = 32
XY = 16
NZ = 16
ATOMS = 128
C = 16
K = 16384
PIECE = 512
PIECES = K // PIECE
TILES = 8
KBS = 4
SLOTS = 64
RAW = 24
GROUP = 8
CHIPS = 8
STEPS = KBS * XY // CHIPS

TWO_PI = 2.0 * math.pi
FORCE_UNIT = 0.001
MAGIC = 12582912.0

SIN_POLY = (-0.79116057, 3.59775961, -7.30781532, 4.44287955)
COS_POLY = (-1.72807912, 5.7151373, -6.97763258, 1.41420395)


def horner(u, poly):
    value = poly[0] * u + poly[1]
    for term in poly[2:]:
        value = value * u + term
    return value


def cos_sin_turns(turns):
    r = turns - ((turns + MAGIC) - MAGIC)
    u = r * r
    s = r * horner(u, SIN_POLY)
    c = horner(u, COS_POLY)
    return 1.0 - s * s, s * c


def dot(a, b, **kw):
    return jnp.dot(a, b, preferred_element_type=f32, **kw)


def dot_nt(a, b):
    return lax.dot_general(a, b, (((1,), (1,)), ((), ())), preferred_element_type=f32)


def kernel(*refs):
    sources, (upd_o, frc_o), held, rest = refs[:14], refs[14:16], refs[16:30], refs[30:]
    feat, pos, wv, fw, wch, win, wout, wup, wlong, sx, sy, nbr, cnt, dist = held
    (W, WA, WB, TA, TB, CS, CR, XS, XR, ZS, ZR, FALL, QS, QP, QA, QB, QC, TAB, GS,
    scr, scr2, base_s, xt_s, qe_s, qf_s, mean_s, env_s, wgt_s, gt_s, wint_s, woutt_s,
    qa_s, qa_r, qb_s, qb_r, qc_s, qc_r, g_s, g_r, c_s, c_r, x_s, x_r, z_s, z_r, f_s, f_r,
    a_s, a_r, b_s, b_r, in_sem) = rest
    loads = [
        pltpu.make_async_copy(sources[n], held[n], in_sem.at[n]) for n in range(14)
    ]
    first_loads = (1, 2, 0, 4)
    later_loads = [n for n in range(14) if n not in first_loads]
    for n in first_loads:
        loads[n].start()
    gx = lax.axis_index("gx")
    gy = lax.axis_index("gy")
    h = lax.rem(gx, 2)
    z = gy // 2
    row, column, xl = gx // 4, lax.rem(gx // 2, 2) * 2 + lax.rem(gy, 2), lax.rem(gy, 2)
    m = row * 4 + column
    sib = (gx + 1 - 2 * h, gy)

    def wrap(i, size):
        return jnp.where(i >= size, i - size, i)

    rows_to = [wrap(row + d, 4) for d in range(4)]
    rows_from = [rows_to[(4 - d) % 4] for d in range(4)]
    columns_to = [wrap(column + d, 4) for d in range(4)]
    columns_from = [columns_to[(4 - d) % 4] for d in range(4)]
    high = [jnp.where(c >= 2, 1, 0) for c in columns_to]
    device_x = [2 * high[d] + h for d in range(4)]
    device_y = [2 * z + columns_to[d] - 2 * high[d] for d in range(4)]
    far_first = (2, 3, 1, 0)

    def xy_to(n):
        if isinstance(n, int):
            return rows_to[far_first[n // 4]] * 4 + columns_to[far_first[n % 4]]
        quarter = jnp.where(n >= 4, 1, 0) + jnp.where(n >= 8, 1, 0) + jnp.where(n >= 12, 1, 0)
        rest = n - 4 * quarter
        dy = jnp.where(quarter < 2, quarter + 2, 3 - quarter)
        dx = jnp.where(rest < 2, rest + 2, 3 - rest)
        return wrap(row + dy, 4) * 4 + wrap(column + dx, 4)

    def xy_from(n):
        return rows_from[far_first[n // 4]] * 4 + columns_from[far_first[n % 4]]

    def xy_dev(n):
        dy, dx = far_first[n // 4], far_first[n % 4]
        return (rows_to[dy] * 4 + device_x[dx], device_y[dx])

    z_far = (8, 7, 9, 6, 10, 5, 11, 4, 12, 3, 13, 2, 14, 1, 15)
    block = lax.rem(z, KBS)

    def z_dev(d):
        return (gx, 2 * wrap(z + d, NZ) + xl)

    x_up = (lax.rem(gx + 1, GX), gy)
    x_down = (lax.rem(gx + GX - 1, GX), gy)
    y_up = (gx, lax.rem(gy + 1, GY))
    y_down = (gx, lax.rem(gy + GY - 1, GY))

    def rcopy(src, dst, ssem, rsem, dev):
        return pltpu.make_async_remote_copy(
            src_ref=src, dst_ref=dst, send_sem=ssem, recv_sem=rsem,
            device_id=dev, device_id_type=pl.DeviceIdType.MESH,
        )

    barrier = pltpu.get_barrier_semaphore()

    def greet(dev):
        pl.semaphore_signal(barrier, inc=1, device_id=dev, device_id_type=pl.DeviceIdType.MESH)

    for n in range(XY - 1):
        greet(z_dev(z_far[n]))
        greet(xy_dev(n))
    greet(sib)
    for dev in (x_up, x_down, y_up, y_down):
        greet(dev)
    for n in later_loads:
        loads[n].start()

    loads[1].wait()
    x3 = pos[...]
    xhi = x3.astype(bf16).astype(f32)
    xmid = (x3 - xhi).astype(bf16).astype(f32)
    xlo = (x3 - xhi) - xmid
    scr2[...] = jnp.zeros_like(scr2)
    scr2[0:3, :] = xhi
    scr2[8:11, :] = xmid
    scr2[16:19, :] = xlo
    xt_s[...] = scr2[...].T.astype(bf16)
    for n in (2, 0, 4):
        loads[n].wait()
    features = feat[...]
    charges_t = dot_nt(wch[...], features).astype(bf16).astype(f32)
    row_id = lax.broadcasted_iota(jnp.int32, (32, ATOMS), 0)
    qf_s[...] = charges_t
    padded = jnp.concatenate([charges_t, jnp.zeros((C, ATOMS), f32)], axis=0)
    qe_s[...] = jnp.where(row_id == C, 1.0, padded).astype(bf16)
    own_sum = jnp.broadcast_to(jnp.sum(charges_t, axis=1, keepdims=True), (C, 128))
    QS[0] = own_sum

    lane_iota = lax.broadcasted_iota(jnp.int32, (ATOMS, 32), 0)

    def pick(list_ref, d, base):
        scr[:, 0:32] = jnp.where(list_ref[d : d + 1, :] == lane_iota + base, 1.0, 0.0)
        return scr[...].T[0:32].astype(bf16)

    ghost = [
        rcopy(GS.at[0], TAB.at[pl.ds(128, 32)], g_s.at[0], g_r.at[0], x_up),
        rcopy(GS.at[1], TAB.at[pl.ds(160, 32)], g_s.at[1], g_r.at[1], x_down),
        rcopy(GS.at[2], TAB.at[pl.ds(192, 32)], g_s.at[2], g_r.at[2], y_up),
        rcopy(GS.at[3], TAB.at[pl.ds(224, 32)], g_s.at[3], g_r.at[3], y_down),
    ]

    qc_copy = rcopy(QS.at[0], QC, qc_s, qc_r, sib)

    def qa_copy(n):
        return rcopy(QP.at[0], QA.at[m], qa_s, qa_r, xy_dev(n))

    qa_all = rcopy(QA.at[pl.ds(0, XY - 1)], QA.at[pl.ds(0, XY - 1)], qa_s, qa_r, sib)

    def qb_copy(n):
        return rcopy(QP.at[1], QB.at[z], qb_s, qb_r, z_dev(z_far[n]))

    qb_all = rcopy(QB.at[pl.ds(0, NZ - 1)], QB.at[pl.ds(0, NZ - 1)], qb_s, qb_r, sib)

    lower = lax.broadcasted_iota(jnp.int32, (C // 2, 128), 1) < 64

    def unpack(packed):
        return jnp.concatenate(
            [jnp.broadcast_to(packed[:, n : n + 1], (C // 2, 128)) for n in (0, 64)], axis=0
        )

    def sum_pair():
        qc_copy.wait_recv()
        pair = QS[0] + QC[...]
        QP[0] = jnp.where(lower, pair[0 : C // 2], pair[C // 2 : C])
        mean_s[...] = jnp.concatenate([pair * (1.0 / (2 * ATOMS))] * KBS, axis=1)

        for n in range(XY - 1):
            qa_copy(n).start()

    def sum_plane():
        qa_all.wait_recv()
        QA[m] = QP[0]
        total = QA[0]
        for j in range(1, XY):
            total = total + QA[j]
        QP[1] = total

        for n in range(NZ - 1):
            qb_copy(n).start()

    def piece_of(n):
        half = jnp.where(n < XY, 1 - h, h)
        return half * XY + xy_to(wrap(n, XY))

    def phases(n, turns):
        first = pl.multiple_of(piece_of(n) * PIECE, PIECE)
        k3 = wv[:, pl.ds(first, PIECE)].astype(f32)
        k8 = jnp.concatenate([k3, jnp.zeros((5, PIECE), f32)], axis=0)
        kb = jnp.concatenate([k8, k8, k8, jnp.zeros((8, PIECE), f32)], axis=0).astype(bf16)
        turns[...] = dot(xt_s[:, 0:32], kb)

    def waves(n, turns, recent):
        g = piece_of(n)
        for j in range(PIECE // 128):
            lanes = slice(j * 128, (j + 1) * 128)
            for p, wave in enumerate(cos_sin_turns(turns[:, lanes])):
                wave = wave.astype(bf16)
                W[g, p, :, lanes] = wave
                recent[p, :, lanes] = wave

    def meet(recent):
        return [dot(qe_s[...], recent[p])[0:RAW] for p in range(2)]

    def core_copy(i):
        return rcopy(CS.at[i], CR.at[i], c_s, c_r.at[i], sib)

    core_all = rcopy(CS, CR, c_s, c_r.at[0], sib)

    def keep_core(n, raw):
        i = xy_to(n)
        CS[i, 0] = raw[0]
        CS[i, 1] = raw[1]

    def xy_copy(i, dev):
        return rcopy(XS.at[i], XR.at[m], x_s, x_r, dev)

    xy_all = rcopy(XR.at[pl.ds(0, XY - 1)], XR.at[pl.ds(0, XY - 1)], x_s, x_r, sib)

    def split_units(units):
        high = units.astype(bf16).astype(f32)
        return jnp.concatenate([high, units - high], axis=0)

    def put_terms(i, raw, keep):
        core_copy(i).wait_recv()
        offset = mean_s[...]
        units = []
        for p in range(2):
            total = raw[p] + CR[i, p]
            unit = total[C : C + 1]
            units.append(unit)
            terms = (total[0:C] - offset * unit).astype(bf16)
            for kb in range(KBS):
                keep[2 * kb + p] = terms[:, kb * 128 : (kb + 1) * 128]
        split = split_units(jnp.concatenate(units, axis=0))
        keep[TILES] = jnp.concatenate(
            [split[:, kb * 128 : (kb + 1) * 128] for kb in range(KBS)], axis=0
        ).astype(bf16)

    def send_xy(n, raw):
        i = xy_to(wrap(n, XY))
        put_terms(i, raw, XS.at[i])
        y = jnp.where(i >= 4, 1, 0) + jnp.where(i >= 8, 1, 0) + jnp.where(i >= 12, 1, 0)
        x = i - 4 * y
        upper = jnp.where(x >= 2, 1, 0)
        xy_copy(i, (4 * y + 2 * upper + h, 2 * z + x - 2 * upper)).start()

    def two_pieces(use):
        def body(step, carry):
            n = 2 * step + 1
            phases(n + 1, TA)
            raw = meet(WA)
            waves(n, TB, WB)
            use(n - 1, raw)
            phases(n + 2, TB)
            raw = meet(WB)
            waves(n + 1, TA, WA)
            use(n, raw)
            return carry

        return body

    phases(0, TA)
    phases(1, TB)
    waves(0, TA, WA)
    lax.fori_loop(0, 8, two_pieces(keep_core), 0)

    pl.semaphore_wait(barrier, 5 + 2 * (XY - 1))

    def start_core(n, carry):
        core_copy(xy_to(n)).start()
        return carry

    qc_copy.start()
    lax.fori_loop(0, 4, start_core, 0)

    for n in later_loads:
        loads[n].wait()
    scr[...] = jnp.zeros_like(scr)
    TAB[0:ATOMS] = features
    for d in range(2):
        GS[d] = dot(pick(sx, d, 0), features).astype(bf16)
    ghost[0].start()
    ghost[1].start()

    sum_pair()
    lax.fori_loop(4, XY, start_core, 0)

    send_two = two_pieces(send_xy)

    def own_half(step, carry):
        pl.when(step == 12)(sum_plane)
        return send_two(step, carry)

    lax.fori_loop(8, 15, own_half, 0)
    raw = meet(WA)
    waves(31, TB, WB)
    send_xy(30, raw)
    put_terms(m, meet(WB), XR.at[m])

    scr2[...] = jnp.zeros_like(scr2)
    scr2[0:20, :] = win[...].astype(f32)
    wint_s[...] = scr2[...].T.astype(bf16)
    woutt_s[...] = wout[...].astype(f32).T.astype(bf16)
    gt_s[:, 0:128] = features.astype(f32).T.astype(bf16)
    slot_id = lax.broadcasted_iota(jnp.int32, (SLOTS, ATOMS), 0)
    swing, _ = cos_sin_turns(dist[...] * 0.1)
    env_s[...] = jnp.where(slot_id < cnt[...], 0.5 * (swing + 1.0), 0.0)

    centre = lax.broadcasted_iota(jnp.int32, (32, ATOMS), 0).astype(f32) * (5.0 / 19.0)
    table_row = lax.broadcasted_iota(jnp.int32, (2 * ATOMS, ATOMS), 0)
    sharpness = 0.02 * 19.0 * 19.0

    def message_step(i, running):
        base = i * GROUP
        basis, hot = [], []
        for u in range(GROUP):
            offset = dist[pl.ds(base + u, 1), :] - centre
            basis.append(jnp.exp(-sharpness * offset * offset).astype(bf16))
            hot.append(jnp.where(nbr[pl.ds(base + u, 1), :] == table_row, 1.0, 0.0).astype(bf16))
        for u in range(0, GROUP, 4):
            pre = dot(wint_s[:, 0:32], jnp.concatenate(basis[u : u + 4], axis=1))
            hidden = jnp.log(0.5 * jnp.exp(pre) + 0.5).astype(bf16)
            filters = dot(woutt_s[...], hidden)
            rows = dot(gt_s[...], jnp.concatenate(hot[u : u + 4], axis=1))
            both = filters * rows
            for v in range(4):
                running = running + env_s[pl.ds(base + u + v, 1), :] * both[:, v * 128 : (v + 1) * 128]
        return running

    ghost[0].wait_recv()
    ghost[1].wait_recv()
    scr[...] = jnp.zeros_like(scr)
    for d in range(2):
        rows = dot(pick(sy, d, 0), TAB[0:128]) + dot(pick(sy, d, 128)[:, 0:64], TAB[128:192])
        GS[2 + d] = rows.astype(bf16)
    ghost[2].start()
    ghost[3].start()

    xy_all.wait_recv()
    pieces = []
    offsets = [unpack(QA[j]) * (1.0 / (2 * ATOMS)) for j in range(XY)]
    for kb in range(KBS):
        totals = [jnp.zeros((C, 128), f32), jnp.zeros((C, 128), f32)]
        units = jnp.zeros((2, 128), f32)
        for j in range(XY):
            parts = XR[j, TILES].astype(f32)
            unit = parts[4 * kb : 4 * kb + 2] + parts[4 * kb + 2 : 4 * kb + 4]
            units = units + unit
            for p in range(2):
                totals[p] = totals[p] + (
                    XR[j, 2 * kb + p].astype(f32) + offsets[j] * unit[p : p + 1]
                )
        pieces.append((totals, units))
    qb_all.wait_recv()
    QB[z] = QP[1]
    mean = QB[0]
    for j in range(1, NZ):
        mean = mean + QB[j]
    mean = unpack(mean) * (1.0 / (GX * GY * ATOMS))
    QS[3] = mean
    for kb, (totals, units) in enumerate(pieces):
        for p in range(2):
            ZS[kb, p] = (totals[p] - mean * units[p : p + 1]).astype(bf16)

    def z_copy(n):
        return rcopy(
            ZS.at[wrap(block + z_far[n] % KBS, KBS)], ZR.at[z], z_s, z_r, z_dev(z_far[n])
        )

    z_all = rcopy(ZR.at[pl.ds(0, NZ - 1)], ZR.at[pl.ds(0, NZ - 1)], z_s, z_r, sib)

    for n in range(NZ - 1):
        z_copy(n).start()
    ZR[z] = ZS[block]

    g_own = h * XY + m
    k_block = pl.multiple_of(g_own * PIECE + block * 128, 128)
    kt = wv[:, pl.ds(k_block, 128)].astype(f32)
    q2 = (TWO_PI * TWO_PI) * (
        kt[0:1] * kt[0:1] + kt[1:2] * kt[1:2] + 0.25 * (kt[2:3] * kt[2:3])
    )
    eye = lax.broadcasted_iota(jnp.int32, (C, C), 0) == lax.broadcasted_iota(jnp.int32, (C, C), 1)
    width = jnp.sum(jnp.where(eye, jnp.broadcast_to(fw[...], (C, C)), 0.0), axis=1, keepdims=True)
    wgt_s[...] = jnp.exp(-0.5 * (width * width) * q2) * ((TWO_PI * TWO_PI) / q2)

    ghost[2].wait_recv()
    ghost[3].wait_recv()
    gt_s[:, 128:256] = TAB[128:256].astype(f32).T.astype(bf16)
    messages = lax.fori_loop(0, SLOTS // GROUP, message_step, jnp.zeros((128, ATOMS), f32))
    message_rows = messages.astype(bf16).astype(f32).T.astype(bf16)
    base_s[...] = features.astype(f32) + dot(message_rows, wup[...])
    scr[...] = jnp.zeros_like(scr)
    scr2[...] = jnp.zeros_like(scr2)
    scr2[0:C, :] = wlong[...]

    qa_all.wait_send()
    qb_all.wait_send()
    qc_copy.wait_send()
    core_all.wait_send()
    xy_all.wait_send()
    for copy in ghost:
        copy.wait_send()

    z_all.wait_recv()
    totals = [jnp.zeros((C, 128), f32), jnp.zeros((C, 128), f32)]
    for j in range(NZ):
        for p in range(2):
            totals[p] = totals[p] + ZR[j, p].astype(f32)
    for p in range(2):
        FALL[g_own, block, p] = (totals[p] * wgt_s[...]).astype(bf16)

    def f_copy(delta, kb, slot):
        return rcopy(
            FALL.at[g_own, kb], FALL.at[g_own, kb], f_s.at[slot], f_r.at[kb],
            z_dev(delta % NZ),
        )

    for n, delta in enumerate((2, 1, -1)):
        f_copy(delta, block, n).start()

    def block_of(turn):
        if isinstance(turn, int):
            return wrap(block + (0, 1, 3, 2)[turn], KBS)
        return wrap(block + jnp.where(turn < 2, turn, 5 - turn), KBS)

    def a_copy(n, turn):
        kb = block_of(turn)
        return rcopy(
            FALL.at[g_own, kb], FALL.at[g_own, kb], a_s, a_r.at[turn * 2 + n // CHIPS],
            xy_dev(n),
        )

    def b_copy(j, turn, group):
        kb = block_of(turn)
        return rcopy(
            FALL.at[h * XY + j, kb], FALL.at[h * XY + j, kb], b_s,
            b_r.at[turn * 2 + group], sib,
        )

    def send_block(turn):
        for n in reversed(range(XY - 1)):
            a_copy(n, turn).start()
        b_copy(m, turn, 1).start()

    send_block(0)
    for turn in range(1, KBS):
        f_copy(1, block_of(turn), 0).wait_recv()
        send_block(turn)
    z_all.wait_send()
    for n in range(3):
        f_copy(1, block, n).wait_send()

    def project(half, group, turn, running):
        kb = block_of(turn)
        f0, f1, kf, w0, w1 = [], [], [], [], []
        for u in range(CHIPS):
            g = half * XY + xy_from(group * CHIPS + u)
            lanes = pl.ds(pl.multiple_of(kb * 128, 128), 128)
            f0.append(FALL[g, kb, 0])
            f1.append(FALL[g, kb, 1])
            kf.append(wv[:, pl.ds(pl.multiple_of(g * PIECE + kb * 128, 128), 128)])
            w0.append(W[g, 0, :, lanes])
            w1.append(W[g, 1, :, lanes])
        f0, f1, kf, w0, w1 = [jnp.concatenate(v, axis=1) for v in (f0, f1, kf, w0, w1)]
        kf = kf.astype(f32) * TWO_PI
        f0w, f1w = f0.astype(f32), f1.astype(f32)
        first, second = [f0], [f1]
        for d in range(3):
            first.append((kf[d : d + 1] * f1w).astype(bf16))
            second.append((-kf[d : d + 1] * f0w).astype(bf16))
        running = running + dot_nt(w0, jnp.concatenate(first, axis=0))
        return running + dot_nt(w1, jnp.concatenate(second, axis=0))

    def wait_near(turn, group):
        chips = FALL.at[pl.ds(0, CHIPS - group), 0]
        rcopy(chips, chips, a_s, a_r.at[turn * 2 + group], sib).wait_recv()
        for u in range(CHIPS - group):
            b_copy(xy_from(group * CHIPS + u), turn, group).start()

    def wait_other(turn, group):
        chips = FALL.at[pl.ds(0, CHIPS), 0]
        rcopy(chips, chips, b_s, b_r.at[turn * 2 + group], sib).wait_recv()

    def first_turn(running):
        for group in (1, 0):
            wait_near(0, group)
            running = project(h, group, 0, running)
        return running

    def next_turn(turn, running):
        for group in (1, 0):
            wait_near(turn, group)
            wait_other(turn - 1, group)
            running = project(h, group, turn, running)
            running = project(1 - h, group, turn - 1, running)
        return running

    def last_turn(running):
        for group in (1, 0):
            wait_other(KBS - 1, group)
            running = project(1 - h, group, KBS - 1, running)
        return running

    fields = first_turn(jnp.zeros((ATOMS, 4 * C), f32))
    fields = lax.fori_loop(1, KBS, next_turn, fields)
    fields = last_turn(fields)

    scr[:, 0 : 4 * C] = fields * (1.0 / math.sqrt(GX * GY * ATOMS))
    columns = scr[...]
    long_part = dot(columns, scr2[...], precision=lax.Precision.HIGHEST)
    rows = columns.T
    centred = qf_s[...] - QS[3]
    for d in range(3):
        part = rows[(d + 1) * C : (d + 2) * C]
        frc_o[d : d + 1, :] = -FORCE_UNIT * jnp.sum(centred * part, axis=0, keepdims=True)
    upd_o[...] = (base_s[...] + long_part).astype(bf16)

    rest_a = FALL.at[pl.ds(0, XY - 1)]
    rcopy(rest_a, rest_a, a_s, a_r.at[0], sib).wait_send()
    rest_b = FALL.at[pl.ds(0, XY)]
    rcopy(rest_b, rest_b, b_s, b_r.at[0], sib).wait_send()


def per_device(*args):
    feat, pos, wv, fw, wch, win, wout, wup, wlong, sx, sy, nbr, cnt, dist = args
    operands = (
        feat, pos, wv, fw.reshape(1, C), wch.T, win, wout, wup, wlong, sx, sy, nbr,
        cnt.reshape(1, ATOMS), dist,
    )
    dma = pltpu.SemaphoreType.DMA
    scratch = [pltpu.VMEM(value.shape, value.dtype) for value in operands] + [
        pltpu.VMEM((PIECES, 2, ATOMS, PIECE), bf16),
        pltpu.VMEM((2, ATOMS, PIECE), bf16),
        pltpu.VMEM((2, ATOMS, PIECE), bf16),
        pltpu.VMEM((ATOMS, PIECE), f32),
        pltpu.VMEM((ATOMS, PIECE), f32),
        pltpu.VMEM((XY, 2, RAW, PIECE), f32),
        pltpu.VMEM((XY, 2, RAW, PIECE), f32),
        pltpu.VMEM((XY, TILES + 1, C, 128), bf16),
        pltpu.VMEM((XY, TILES + 1, C, 128), bf16),
        pltpu.VMEM((KBS, 2, C, 128), bf16),
        pltpu.VMEM((NZ, 2, C, 128), bf16),
        pltpu.VMEM((PIECES, KBS, 2, C, 128), bf16),
        pltpu.VMEM((4, C, 128), f32),
        pltpu.VMEM((2, C // 2, 128), f32),
        pltpu.VMEM((XY, C // 2, 128), f32),
        pltpu.VMEM((NZ, C // 2, 128), f32),
        pltpu.VMEM((C, 128), f32),
        pltpu.VMEM((2 * ATOMS, 128), bf16),
        pltpu.VMEM((4, 32, 128), bf16),
        pltpu.VMEM((128, 128), f32),
        pltpu.VMEM((128, 128), f32),
        pltpu.VMEM((128, 128), f32),
        pltpu.VMEM((128, 128), bf16),
        pltpu.VMEM((32, ATOMS), bf16),
        pltpu.VMEM((C, ATOMS), f32),
        pltpu.VMEM((C, PIECE), f32),
        pltpu.VMEM((SLOTS, ATOMS), f32),
        pltpu.VMEM((C, 128), f32),
        pltpu.VMEM((128, 256), bf16),
        pltpu.VMEM((128, 128), bf16),
        pltpu.VMEM((128, 128), bf16),
        dma, dma, dma, dma, dma, dma,
        dma((4,)), dma((4,)),
        dma, dma((XY,)),
        dma, dma,
        dma, dma,
        dma((KBS,)), dma((KBS,)),
        dma, dma((STEPS,)),
        dma, dma((STEPS,)),
        dma((14,)),
    ]
    vmem = pl.BlockSpec(memory_space=pltpu.VMEM)
    return pl.pallas_call(
        kernel,
        out_shape=(
            jax.ShapeDtypeStruct((ATOMS, 128), bf16),
            jax.ShapeDtypeStruct((3, ATOMS), f32),
        ),
        in_specs=[pl.BlockSpec(memory_space=pl.ANY)] * 14,
        out_specs=(vmem, vmem),
        scratch_shapes=scratch,
        compiler_params=pltpu.CompilerParams(
            collective_id=0, has_side_effects=True, vmem_limit_bytes=56 * 1024 * 1024
        ),
    )(*operands)


def solution(mesh):
    atoms_first = P(("gx", "gy"), None)
    atoms_last = P(None, ("gx", "gy"))
    placed = (
        atoms_first, atoms_last, P(), P(), P(), P(), P(), P(), P(),
        atoms_last, atoms_last, atoms_last, P(("gx", "gy")), atoms_last,
    )
    return jax.shard_map(
        per_device,
        mesh=mesh,
        in_specs=placed,
        out_specs=(atoms_first, atoms_last),
        check_vma=False,
    )
```
